128 devices in a mesh: dom: 32 (over x, z, core), rep: 4 (over y).
Axes of the slice: x: 4, y: 4, z: 4, core: 2. Of those that a mesh axis runs over, the one named last changes fastest.
Arguments:
- features: bfloat16 [131072, 128], P(('dom', 'rep')), may hold values from -6 to 6
- adjacency: bfloat16 [131072, 1024], P(('dom', 'rep')), may hold values from -0.09375 to 0.09375
- halo_weights: bfloat16 [131072, 3072], P(('dom', 'rep')), may hold values from -0.09375 to 0.09375
- history: bfloat16 [2, 131072, 256], P(None, ('dom', 'rep')), may hold values from -6 to 6
- pull_ids: int32 [16384, 24], P(('dom', 'rep')), may hold values from 0 to 1023
- pull_count: int32 [128, 128], P(('dom', 'rep')), may hold values from 0 to 24, as said below
- w_in: bfloat16 [128, 256], replicated, may hold values from -0.5 to 0.5
- w_layers: bfloat16 [2, 256, 256], replicated, may hold values from -0.375 to 0.375
- cotangent: float32 [131072, 256], P(('dom', 'rep')), may hold values from -96 to 96
Outputs:
- final_out: bfloat16 [131072, 256], P(('dom', 'rep'))
- fresh_history: bfloat16 [2, 131072, 256], P(None, ('dom', 'rep'))
- grad_in: float32 [128, 256], replicated
- grad_layers: float32 [2, 256, 256], replicated
The draws below stay inside these ranges and needn't reach their ends.
Inputs may be any that keep to these rules, and one draw needn't show every extreme that they name: pull_count[r, o] is 0 where o == r, and every requester r has some owner with exactly 24 live slots; slots beyond the count hold valid but unused row ids.
All inputs are finite; a program needn't handle non-finite values.
Results may differ from the reference program's by a relative error of at most 0.012.
Values may be sent and summed in bfloat16 or wider, within the bound.
A program may use at most 64 MiB of HBM per device.

```python
import math
import jax
import jax.numpy as jnp
from jax import lax

F = 256
FIN = 128
LAYERS = 2
ROWS_DEV = 1024
CAP = 24
NODES = 131072
HALO = 3072
DEVICES = 128


def draw_pull_count(key, part):
    key = jax.random.fold_in(key, 11)
    subkeys = jax.random.split(key, 4)
    hot_pairs = jax.random.randint(subkeys[0], (DEVICES, DEVICES), 0, 4) == 0
    heavy_load = jax.random.randint(subkeys[1], (DEVICES, DEVICES), CAP // 2, CAP + 1)
    light_load = jax.random.randint(subkeys[2], (DEVICES, DEVICES), 1, CAP // 3 + 1)
    counts = jnp.where(hot_pairs, heavy_load, light_load)
    device_ids = jnp.arange(DEVICES, dtype=jnp.int32)
    offset = jax.random.randint(subkeys[3], (DEVICES,), 1, DEVICES)
    chosen = (device_ids + offset) % DEVICES
    counts = jnp.where(device_ids[None, :] == chosen[:, None], CAP, counts)
    counts = jnp.where(device_ids[None, :] == device_ids[:, None], 0, counts)
    return counts.astype(jnp.int32)


def draw_cotangent(key, part):
    key = jax.random.fold_in(key, 23)
    subkeys = jax.random.split(key, 2)
    base = jnp.clip(jax.random.normal(subkeys[0], (NODES, F), jnp.float32), -6.0, 6.0)
    heavy_count = max(2, DEVICES // 32)
    order = jax.random.permutation(subkeys[1], DEVICES)
    cluster_scale = jnp.where(order < heavy_count, 16.0, 1.0).astype(jnp.float32)
    scaled = base.reshape(DEVICES, ROWS_DEV, F) * cluster_scale[:, None, None]
    return scaled.reshape(NODES, F).astype(jnp.float32)


def plant(values, own_key, low, largest):
    extent = values.shape
    place = [jax.random.randint(jax.random.fold_in(own_key, axis), (), 0, extent[axis]) for axis in range(len(extent))]
    values = values.at[tuple(place)].set(low)
    longest = extent.index(max(extent))
    place[longest] = (place[longest] + 1) % extent[longest]
    return values.at[tuple(place)].set(largest)


def levels(stream_key, shape, shards, low, largest):
    def one(dim, blocks):
        draws = jax.random.uniform(jax.random.fold_in(jax.random.fold_in(stream_key, 6), dim), (blocks,), jnp.float32, low / len(shards), largest / len(shards))
        return jnp.repeat(jnp.exp(draws), shape[dim] // blocks).reshape((-1,) + (1,) * (len(shape) - dim - 1))

    level = one(*shards[0])
    for cut in shards[1:]:
        level = level * one(*cut)
    return level


def centred(rng, shape, width, limit, cuts=(), held_as=jnp.bfloat16):
    loudness = levels(rng, shape, cuts, -0.22, 0.18) if cuts else 1.0
    array = jax.random.normal(rng, shape, jnp.float32) * width * loudness
    return jnp.minimum(jnp.maximum(array, -limit), limit).astype(held_as)


def setup_inputs(seed: int = 0) -> dict:
    key_list = jax.random.split(jax.random.key(seed), 10)
    features = centred(key_list[0], (NODES, FIN), 1.0, 6.0, ((0, 128),))
    adjacency = centred(key_list[1], (NODES, ROWS_DEV), (ROWS_DEV + HALO) ** -0.5, 0.09375, ((0, 128),))
    halo_weights = centred(key_list[2], (NODES, HALO), (ROWS_DEV + HALO) ** -0.5, 0.09375, ((0, 128),))
    history = centred(key_list[3], (LAYERS, NODES, F), 1.0, 6.0, ((1, 128),))
    pull_ids = plant(jax.random.randint(key_list[4], (DEVICES * DEVICES, CAP), 0, ROWS_DEV), jax.random.fold_in(key_list[4], 1), 0, ROWS_DEV - 1).astype(jnp.int32)
    pull_count = draw_pull_count(jax.random.fold_in(key_list[9], 71), 0)
    w_in = centred(key_list[6], (FIN, F), FIN ** -0.5, 0.5)
    w_layers = centred(key_list[7], (LAYERS, F, F), F ** -0.5, 0.375)
    cotangent = draw_cotangent(jax.random.fold_in(key_list[9], 71), 0)
    return dict(features=features, adjacency=adjacency, halo_weights=halo_weights, history=history, pull_ids=pull_ids, pull_count=pull_count, w_in=w_in, w_layers=w_layers, cotangent=cotangent)


RESTART = 0.1
DECAY_RATE = 0.5

def silu_slope(value):
    sig = jax.nn.sigmoid(value)
    return sig * (1.0 + value * (1.0 - sig))

def local_step(node_feats, adj_block, halo_block, pulled_rows, w_in, w_layers, cot_block):
    pre_input = jnp.dot(node_feats, w_in, preferred_element_type=jnp.float32)
    initial = jax.nn.silu(pre_input).astype(jnp.bfloat16)
    current = initial
    stored = []
    refreshed = [initial]
    layers = w_layers.shape[0]
    for layer_idx in range(layers):
        mix_rate = math.log(DECAY_RATE / (layer_idx + 1) + 1.0)
        neighbour_sum = jnp.dot(adj_block, current, preferred_element_type=jnp.float32) + jnp.dot(halo_block, pulled_rows[layer_idx], preferred_element_type=jnp.float32)
        combined = (1.0 - RESTART) * neighbour_sum + RESTART * initial.astype(jnp.float32)
        combined_bf = combined.astype(jnp.bfloat16)
        pre_act = (1.0 - mix_rate) * combined + mix_rate * jnp.dot(combined_bf, w_layers[layer_idx], preferred_element_type=jnp.float32)
        stored.append((combined_bf, pre_act))
        current = jax.nn.silu(pre_act).astype(jnp.bfloat16)
        if layer_idx + 1 < layers:
            refreshed.append(current)
    grad_state = cot_block
    grad_init = jnp.zeros(cot_block.shape, jnp.float32)
    grad_list = [None] * layers
    for layer_idx in reversed(range(layers)):
        mix_rate = math.log(DECAY_RATE / (layer_idx + 1) + 1.0)
        combined_bf, pre_act = stored[layer_idx]
        grad_pre = grad_state * silu_slope(pre_act)
        grad_bf = grad_pre.astype(jnp.bfloat16)
        grad_list[layer_idx] = mix_rate * jnp.dot(combined_bf.T, grad_bf, preferred_element_type=jnp.float32)
        grad_comb = (1.0 - mix_rate) * grad_pre + mix_rate * jnp.dot(grad_bf, w_layers[layer_idx].T, preferred_element_type=jnp.float32)
        grad_init = grad_init + RESTART * grad_comb
        grad_state = (1.0 - RESTART) * jnp.dot(adj_block.T, grad_comb.astype(jnp.bfloat16), preferred_element_type=jnp.float32)
    grad_first = (grad_init + grad_state) * silu_slope(pre_input)
    grad_proj = jnp.dot(node_feats.T, grad_first.astype(jnp.bfloat16), preferred_element_type=jnp.float32)
    return (current, jnp.stack(refreshed), grad_proj, jnp.stack(grad_list))

def reference(features, adjacency, halo_weights, history, pull_ids, pull_count, w_in, w_layers, cotangent):
    devices = DEVICES
    feat_all = features.reshape(devices, ROWS_DEV, FIN)
    adj_all = adjacency.reshape(devices, ROWS_DEV, ROWS_DEV)
    halo_all = halo_weights.reshape(devices, ROWS_DEV, HALO)
    hist_all = history.reshape(LAYERS, devices, ROWS_DEV, F)
    id_all = pull_ids.reshape(devices, devices, CAP).astype(jnp.int32)
    cot_all = cotangent.reshape(devices, ROWS_DEV, F)
    owners = jnp.arange(devices, dtype=jnp.int32)[:, None]
    slot_idx = jnp.arange(CAP, dtype=jnp.int32)[None, :]

    def per_device(device):
        row_ids = id_all[device]
        pulled = hist_all[:, owners, row_ids]
        valid_mask = slot_idx < pull_count[device].astype(jnp.int32)[:, None]
        pulled = jnp.where(valid_mask[None, :, :, None], pulled, jnp.zeros((), pulled.dtype)).reshape(LAYERS, HALO, F)
        return local_step(feat_all[device], adj_all[device], halo_all[device], pulled, w_in, w_layers, cot_all[device])
    results = lax.map(per_device, jnp.arange(devices, dtype=jnp.int32))
    final_out = results[0].reshape(NODES, F)
    fresh_history = jnp.transpose(results[1], (1, 0, 2, 3)).reshape(LAYERS, NODES, F)
    factor = 1.0 / math.sqrt(NODES)
    grad_in = lax.optimization_barrier(jnp.sum(results[2], axis=0)) * factor
    grad_layers = lax.optimization_barrier(jnp.sum(results[3], axis=0)) * factor
    return (final_out, fresh_history, grad_in, grad_layers)
```

```python
import functools
import math
import random

import jax
import jax.numpy as jnp
from jax import lax
from jax.experimental import pallas as pl
from jax.experimental.pallas import tpu as pltpu
from jax.sharding import PartitionSpec as P

RESTART = 0.1
DECAY_RATE = 0.5
MESH = pl.DeviceIdType.MESH
BF = jnp.bfloat16
F32 = jnp.float32

ROWS = 1024
WIDTH = 256
FIN = 128
SLOTS = 24
DEVICES = 128
HALO = DEVICES * SLOTS
TILE = 256
GROUP = 16
UNITS = 32

ORDER = [(k // 32, k % 4, (k // 8) % 4, (k // 4) % 2) for k in range(1, DEVICES)]
random.Random(4).shuffle(ORDER)
MIX = [math.log(DECAY_RATE / (layer + 1) + 1.0) for layer in range(2)]


def mm(a, b):
    return jnp.dot(a, b, preferred_element_type=F32)


def slope(value, sig):
    return sig * (1.0 + value * (1.0 - sig))


def kernel(
    feat_h, adj_h, halo_h, hist_h, ids_h, cnt_h, win_h, wl_h, cot_h,
    final_h, fresh_h, gsum,
    feat, adj, halo, hist, ids, cnt, win, wl, cot,
    idsend, idrecv, idcol, send, recv, pulled,
    init, x1, fin, adj_t, feat_t, wl_t, cb0_t,
    slope_in, slope0, base, ginit, gcb, gl, grad, rsbuf, unit,
    in_sem, out_sem, id_send, id_recv, row_send, row_recv, rs_send, rs_recv, ag_send, ag_recv,
):
    dom, y = lax.axis_index("dom"), lax.axis_index("rep")
    x, z, core = dom // 8, (dom // 2) % 4, dom % 2
    me = dom * 4 + y
    fwd_x = [(x + d) % 4 * 8 for d in range(4)]
    fwd_z = [(z + d) % 4 * 2 for d in range(4)]
    fwd_y = [(y + d) % 4 for d in range(4)]
    cores = [core, 1 - core]

    def ahead(off):
        return (fwd_x[off[0]] + fwd_z[off[2]] + cores[off[3]], fwd_y[off[1]])

    def behind(off):
        return (
            fwd_x[(4 - off[0]) % 4] + fwd_z[(4 - off[2]) % 4] + cores[off[3]],
            fwd_y[(4 - off[1]) % 4],
        )

    idrecv[pl.ds(DEVICES - 1, 1), :] = jnp.full((1, DEVICES), -1, jnp.int32)
    barrier = pltpu.get_barrier_semaphore()
    for off in ORDER:
        pl.semaphore_signal(barrier, inc=1, device_id=ahead(off), device_id_type=MESH)

    loads = [
        pltpu.make_async_copy(src, dst, in_sem.at[i])
        for i, (src, dst) in enumerate(
            [
                (ids_h, ids), (cnt_h, cnt), (hist_h, hist), (feat_h, feat), (win_h, win),
                (wl_h, wl), (adj_h, adj), (halo_h, halo), (cot_h, cot),
            ]
        )
    ]
    for load in loads:
        load.start()

    loads[0].wait()
    loads[1].wait()
    slot = lax.broadcasted_iota(jnp.int32, (SLOTS, DEVICES), 0)
    wanted = jnp.where(slot < cnt[...], ids[...], -1)
    wanted = jnp.concatenate([wanted, jnp.full((DEVICES - SLOTS, DEVICES), -1, jnp.int32)], axis=0)
    idsend[...] = wanted.T

    pl.semaphore_wait(barrier, DEVICES - 1)
    for p, off in enumerate(ORDER):
        to = behind(off)
        pltpu.make_async_remote_copy(
            src_ref=idsend.at[pl.ds(to[0] * 4 + to[1], 1)], dst_ref=idrecv.at[pl.ds(p, 1)],
            send_sem=id_send, recv_sem=id_recv, device_id=to, device_id_type=MESH,
        ).start()
    recv[0, me] = jnp.zeros((2 * SLOTS, 128), BF)
    recv[1, me] = jnp.zeros((2 * SLOTS, 128), BF)
    loads[2].wait()
    ids_all = pltpu.make_async_copy(
        idrecv.at[pl.ds(0, DEVICES - 1)], idrecv.at[pl.ds(0, DEVICES - 1)], id_recv
    )
    ids_all.wait()

    idcol[...] = idrecv[...].T

    def row_copy(layer, p):
        return pltpu.make_async_remote_copy(
            src_ref=send.at[layer, p], dst_ref=recv.at[layer, me],
            send_sem=row_send.at[layer], recv_sem=row_recv.at[layer],
            device_id=ahead(ORDER[p]), device_id_type=MESH,
        )

    row_id = lax.broadcasted_iota(jnp.int32, (SLOTS, ROWS), 1)
    for first in range(0, DEVICES - 1, GROUP):
        part = range(first, min(first + GROUP, DEVICES - 1))
        one_hot = jnp.concatenate(
            [
                jnp.where(idcol[pl.ds(0, SLOTS), pl.ds(p, 1)] == row_id, 1.0, 0.0).astype(BF)
                for p in part
            ],
            axis=0,
        )
        for layer in range(2):
            rows = mm(one_hot, hist[layer]).astype(BF)
            for i, p in enumerate(part):
                mine = rows[i * SLOTS : (i + 1) * SLOTS]
                send[layer, p] = jnp.concatenate([mine[:, :128], mine[:, 128:]], axis=0)
            if layer == 0:
                for p in part:
                    row_copy(0, p).start()
    for p in range(DEVICES - 1):
        row_copy(1, p).start()

    for load in loads[3:7]:
        load.wait()
    for layer in range(2):
        wl_t[layer] = wl[layer].T
    feat_t[...] = feat[...].T

    @pl.loop(0, ROWS // TILE)
    def _(t):
        here = pl.ds(pl.multiple_of(t * TILE, TILE), TILE)
        pre = mm(feat[here, :], win[...])
        sig = jax.nn.sigmoid(pre)
        init[here, :] = (pre * sig).astype(BF)
        slope_in[here, :] = slope(pre, sig)
        adj_t[:, here] = adj[here, :].T

    fresh0 = pltpu.make_async_copy(init, fresh_h.at[0], out_sem.at[0])
    fresh0.start()

    def neighbours(state):
        @pl.loop(0, ROWS // TILE)
        def _(t):
            here = pl.ds(pl.multiple_of(t * TILE, TILE), TILE)
            base[here, :] = (1.0 - RESTART) * mm(adj[here, :], state[...]) + RESTART * init[
                here, :
            ].astype(F32)

    def unpack(layer):
        @pl.loop(0, DEVICES // 2)
        def _(o):
            both = [recv[layer, 2 * o], recv[layer, 2 * o + 1]]
            both = [jnp.concatenate([b[:SLOTS], b[SLOTS:]], axis=1) for b in both]
            rows = pl.ds(pl.multiple_of(o * 2 * SLOTS, 2 * SLOTS), 2 * SLOTS)
            pulled[rows, :] = jnp.concatenate(both, axis=0)

    def row_wait(layer):
        got = recv.at[layer, pl.ds(0, DEVICES - 1)]
        pltpu.make_async_copy(got, got, row_recv.at[layer]).wait()

    neighbours(init)
    loads[7].wait()
    loads[8].wait()
    row_wait(0)
    unpack(0)

    @pl.loop(0, ROWS // TILE)
    def _(t):
        here = pl.ds(pl.multiple_of(t * TILE, TILE), TILE)
        comb = base[here, :] + (1.0 - RESTART) * mm(halo[here, :], pulled[...])
        comb_bf = comb.astype(BF)
        cb0_t[:, here] = comb_bf.T
        pre = (1.0 - MIX[0]) * comb + MIX[0] * mm(comb_bf, wl[0])
        sig = jax.nn.sigmoid(pre)
        x1[here, :] = (pre * sig).astype(BF)
        slope0[here, :] = slope(pre, sig)

    fresh1 = pltpu.make_async_copy(x1, fresh_h.at[1], out_sem.at[1])
    fresh1.start()
    neighbours(x1)
    row_wait(1)
    unpack(1)

    gl[...] = jnp.zeros_like(gl)

    @pl.loop(0, ROWS // TILE)
    def _(t):
        here = pl.ds(pl.multiple_of(t * TILE, TILE), TILE)
        comb = base[here, :] + (1.0 - RESTART) * mm(halo[here, :], pulled[...])
        comb_bf = comb.astype(BF)
        pre = (1.0 - MIX[1]) * comb + MIX[1] * mm(comb_bf, wl[1])
        sig = jax.nn.sigmoid(pre)
        fin[here, :] = (pre * sig).astype(BF)
        g_pre = cot[here, :] * slope(pre, sig)
        e = g_pre.astype(BF)
        gl[...] += mm(comb_bf.T, e)
        g_comb = (1.0 - MIX[1]) * g_pre + MIX[1] * mm(e, wl_t[1])
        ginit[here, :] = RESTART * g_comb
        gcb[0, here, :] = g_comb.astype(BF)

    final = pltpu.make_async_copy(fin, final_h, out_sem.at[2])
    final.start()

    def owner(part, u):
        if part < 2:
            return (u, (u // 8 + (u // 2) % 4 + part) % 4)
        return (2 * u, (u // 4 + u % 4 + 2) % 4)

    def place(part, u):
        blocks = 16 if part < 2 else 8
        start = WIDTH * part + (u % blocks) * 16
        return pl.ds(pl.multiple_of(start, 16), 16), pl.ds(pl.multiple_of(u // blocks * 128, 128), 128)

    def scatter(part):
        count = UNITS if part < 2 else UNITS // 2

        @pl.loop(0, count)
        def _(i):
            u = (i + dom + 8 * y) % count
            to = owner(part, u)
            rows, lanes = place(part, u)
            own = (to[0] == dom) & (to[1] == y)

            @pl.when(own)
            def _():
                rsbuf[me] = grad[rows, lanes]

            @pl.when(jnp.logical_not(own))
            def _():
                pltpu.make_async_remote_copy(
                    src_ref=grad.at[rows, lanes], dst_ref=rsbuf.at[me],
                    send_sem=rs_send, recv_sem=rs_recv, device_id=to, device_id_type=MESH,
                ).start()

    grad[pl.ds(0, WIDTH), :] = (MIX[1] * gl[...]).astype(BF)
    scatter(0)
    gl[...] = jnp.zeros_like(gl)

    @pl.loop(0, ROWS // TILE)
    def _(t):
        here = pl.ds(pl.multiple_of(t * TILE, TILE), TILE)
        g_state = (1.0 - RESTART) * mm(adj_t[here, :], gcb[0])
        g_pre = g_state * slope0[here, :]
        e = g_pre.astype(BF)
        gl[...] += mm(cb0_t[:, here], e)
        g_comb = (1.0 - MIX[0]) * g_pre + MIX[0] * mm(e, wl_t[0])
        ginit[here, :] += RESTART * g_comb
        gcb[1, here, :] = g_comb.astype(BF)

    grad[pl.ds(WIDTH, WIDTH), :] = (MIX[0] * gl[...]).astype(BF)
    scatter(1)
    gl[pl.ds(0, FIN), :] = jnp.zeros((FIN, WIDTH), F32)

    @pl.loop(0, ROWS // TILE)
    def _(t):
        here = pl.ds(pl.multiple_of(t * TILE, TILE), TILE)
        g_state = (1.0 - RESTART) * mm(adj_t[here, :], gcb[1])
        g_first = (ginit[here, :] + g_state) * slope_in[here, :]
        gl[pl.ds(0, FIN), :] += mm(feat_t[:, here], g_first.astype(BF))

    grad[pl.ds(2 * WIDTH, FIN), :] = gl[pl.ds(0, FIN), :].astype(BF)
    scatter(2)

    turn = (y - x - z + 8) % 4
    has_unit = (turn < 2) | ((turn == 2) & (core == 0))

    @pl.when(has_unit)
    def _():
        got = rsbuf.at[pl.ds(0, DEVICES - 1)]
        pltpu.make_async_copy(got, got, rs_recv).wait()
        unit[...] = jnp.sum(rsbuf[...].astype(F32), axis=0).astype(BF)
        blocks = jnp.where(turn < 2, 16, 8)
        u = jnp.where(turn < 2, dom, dom // 2)
        rows = pl.ds(pl.multiple_of(WIDTH * turn + (u % blocks) * 16, 16), 16)
        lanes = pl.ds(pl.multiple_of(u // blocks * 128, 128), 128)
        gsum[rows, lanes] = unit[...]
        for off in ORDER:
            pltpu.make_async_remote_copy(
                src_ref=unit, dst_ref=gsum.at[rows, lanes],
                send_sem=ag_send, recv_sem=ag_recv, device_id=ahead(off), device_id_type=MESH,
            ).start()

    def drain(ref, sem):
        pltpu.make_async_copy(ref, ref, sem).wait()

    @pl.when(jnp.logical_not(has_unit))
    def _():
        drain(rsbuf.at[pl.ds(0, 80)], rs_send)
        drain(rsbuf.at[pl.ds(0, 80)], ag_recv)

    @pl.when(has_unit)
    def _():
        drain(rsbuf.at[pl.ds(0, 79)], rs_send)
        drain(rsbuf.at[pl.ds(0, 79)], ag_recv)
        drain(rsbuf.at[pl.ds(0, DEVICES - 1)], ag_send)

    drain(idsend.at[pl.ds(0, DEVICES - 1)], id_send)
    drain(send.at[0, pl.ds(0, DEVICES - 1)], row_send.at[0])
    drain(send.at[1, pl.ds(0, DEVICES - 1)], row_send.at[1])
    fresh0.wait()
    fresh1.wait()
    final.wait()


def local(
    features, adjacency, halo_weights, history, pull_ids, pull_count, w_in, w_layers, cotangent
):
    hbm = pl.BlockSpec(memory_space=pl.ANY)
    vmem = pltpu.VMEM
    dma = pltpu.SemaphoreType.DMA
    final_out, fresh, gsum = pl.pallas_call(
        kernel,
        out_shape=(
            jax.ShapeDtypeStruct((ROWS, WIDTH), BF),
            jax.ShapeDtypeStruct((2, ROWS, WIDTH), BF),
            jax.ShapeDtypeStruct((2 * WIDTH + FIN, WIDTH), BF),
        ),
        in_specs=[hbm] * 9,
        out_specs=(hbm, hbm, pl.BlockSpec(memory_space=vmem)),
        scratch_shapes=[
            vmem((ROWS, FIN), BF),
            vmem((ROWS, ROWS), BF),
            vmem((ROWS, HALO), BF),
            vmem((2, ROWS, WIDTH), BF),
            vmem((SLOTS, DEVICES), jnp.int32),
            vmem((1, DEVICES), jnp.int32),
            vmem((FIN, WIDTH), BF),
            vmem((2, WIDTH, WIDTH), BF),
            vmem((ROWS, WIDTH), F32),
            vmem((DEVICES, 128), jnp.int32),
            vmem((DEVICES, 128), jnp.int32),
            vmem((128, DEVICES), jnp.int32),
            vmem((2, DEVICES, 2 * SLOTS, 128), BF),
            vmem((2, DEVICES, 2 * SLOTS, 128), BF),
            vmem((HALO, WIDTH), BF),
            vmem((ROWS, WIDTH), BF),
            vmem((ROWS, WIDTH), BF),
            vmem((ROWS, WIDTH), BF),
            vmem((ROWS, ROWS), BF),
            vmem((FIN, ROWS), BF),
            vmem((2, WIDTH, WIDTH), BF),
            vmem((WIDTH, ROWS), BF),
            vmem((ROWS, WIDTH), F32),
            vmem((ROWS, WIDTH), F32),
            vmem((ROWS, WIDTH), F32),
            vmem((ROWS, WIDTH), F32),
            vmem((2, ROWS, WIDTH), BF),
            vmem((WIDTH, WIDTH), F32),
            vmem((2 * WIDTH + FIN, WIDTH), BF),
            vmem((DEVICES, 16, 128), BF),
            vmem((16, 128), BF),
            dma((9,)),
            dma((3,)),
            dma(()),
            dma(()),
            dma((2,)),
            dma((2,)),
            dma(()),
            dma(()),
            dma(()),
            dma(()),
        ],
        compiler_params=pltpu.CompilerParams(
            collective_id=0, has_side_effects=True, vmem_limit_bytes=48 * 2**20
        ),
    )(
        features, adjacency, halo_weights, history, pull_ids.T, pull_count, w_in, w_layers, cotangent
    )
    factor = 1.0 / math.sqrt(ROWS * DEVICES)
    sums = gsum.astype(F32) * factor
    layers = jnp.stack([sums[WIDTH : 2 * WIDTH], sums[:WIDTH]])
    return (final_out, fresh, sums[2 * WIDTH :], layers)


def solution(mesh):
    rows = P(("dom", "rep"), None)
    history = P(None, ("dom", "rep"), None)
    return jax.shard_map(
        local,
        mesh=mesh,
        in_specs=(rows, rows, rows, history, rows, rows, P(), P(), rows),
        out_specs=(rows, history, P(), P()),
        check_vma=False,
    )
```

```python
import functools
import math
import random

import jax
import jax.numpy as jnp
from jax import lax
from jax.experimental import pallas as pl
from jax.experimental.pallas import tpu as pltpu
from jax.sharding import PartitionSpec as P

RESTART = 0.1
DECAY_RATE = 0.5
MESH = pl.DeviceIdType.MESH
BF = jnp.bfloat16
F32 = jnp.float32

ROWS = 1024
WIDTH = 256
FIN = 128
SLOTS = 24
DEVICES = 128
HALO = DEVICES * SLOTS
TILE = 512
GROUP = 16
VMEM_LIMIT = 64 * 2**20


def shuffled(offsets, seed):
    offsets = list(offsets)
    random.Random(seed).shuffle(offsets)
    return offsets


OFFSETS = [(k // 32, k % 4, (k // 8) % 4, (k // 4) % 2) for k in range(1, DEVICES)]
ORDER = shuffled(OFFSETS, 4)
EARLY, LATE = (1, 3), (0, 2)
ORDER_LATER = shuffled([o for o in ORDER if o[0] in EARLY], 5) + shuffled(
    [o for o in ORDER if o[0] in LATE], 6
)
PLANE = shuffled([o for o in OFFSETS if o[1] == 0 and o[3] == 0], 7)
CREW = shuffled([o for o in OFFSETS if o[0] == 0 and o[2] == 0], 8)
MIX = [math.log(DECAY_RATE / (layer + 1) + 1.0) for layer in range(2)]


def mm(a, b):
    return jnp.dot(a, b, preferred_element_type=F32)


def slope(value, sig):
    return sig * (1.0 + value * (1.0 - sig))


def kernel(
    feat_h, adj_h, halo_h, hist_h, ids_h, cnt_h, win_h, wl_h, cot_h,
    final_h, fresh_h, gsum,
    feat, adj, halo, hist, ids, cnt, win, wl, cot,
    idsend, idrecv, idcol, send, recv, pulled,
    init, x1, fin, adj_t, feat_t, wl_t, cb0_t,
    slope_in, slope0, base, ginit, gcb, gl, grad, plane_buf, crew_buf,
    in_sem, out_sem, id_send, id_recv, row_send, row_recv, sum_send, sum_recv,
):
    dom, y = lax.axis_index("dom"), lax.axis_index("rep")
    x, z, core = dom // 8, (dom // 2) % 4, dom % 2
    me = dom * 4 + y
    fwd_x = [(x + d) % 4 * 8 for d in range(4)]
    fwd_z = [(z + d) % 4 * 2 for d in range(4)]
    fwd_y = [(y + d) % 4 for d in range(4)]
    cores = [core, 1 - core]

    def ahead(off):
        return (fwd_x[off[0]] + fwd_z[off[2]] + cores[off[3]], fwd_y[off[1]])

    def behind(off):
        return (
            fwd_x[(4 - off[0]) % 4] + fwd_z[(4 - off[2]) % 4] + cores[off[3]],
            fwd_y[(4 - off[1]) % 4],
        )

    def drain(ref, sem):
        pltpu.make_async_copy(ref, ref, sem).wait()

    idrecv[pl.ds(DEVICES - 1, 1), :] = jnp.full((1, DEVICES), -1, jnp.int32)
    barrier = pltpu.get_barrier_semaphore()
    for off in ORDER:
        pl.semaphore_signal(barrier, inc=1, device_id=ahead(off), device_id_type=MESH)

    loads = [
        pltpu.make_async_copy(src, dst, in_sem.at[i])
        for i, (src, dst) in enumerate(
            [
                (ids_h, ids), (cnt_h, cnt), (hist_h, hist), (feat_h, feat), (win_h, win),
                (wl_h, wl), (adj_h, adj), (halo_h, halo), (cot_h, cot),
            ]
        )
    ]
    for load in loads:
        load.start()

    loads[0].wait()
    loads[1].wait()
    slot = lax.broadcasted_iota(jnp.int32, (SLOTS, DEVICES), 0)
    wanted = jnp.where(slot < cnt[...], ids[...], -1)
    wanted = jnp.concatenate([wanted, jnp.full((DEVICES - SLOTS, DEVICES), -1, jnp.int32)], axis=0)
    idsend[...] = wanted.T

    pl.semaphore_wait(barrier, DEVICES - 1)
    groups = [
        range(first, min(first + GROUP, DEVICES - 1)) for first in range(0, DEVICES - 1, GROUP)
    ]

    for p, off in enumerate(ORDER):
        to = behind(off)
        pltpu.make_async_remote_copy(
            src_ref=idsend.at[pl.ds(to[0] * 4 + to[1], 1)], dst_ref=idrecv.at[pl.ds(p, 1)],
            send_sem=id_send, recv_sem=id_recv, device_id=to, device_id_type=MESH,
        ).start()
    recv[0, me] = jnp.zeros((2 * SLOTS, 128), BF)
    recv[1, me] = jnp.zeros((2 * SLOTS, 128), BF)
    loads[2].wait()

    def row_copy(layer, off):
        return pltpu.make_async_remote_copy(
            src_ref=send.at[layer, ORDER.index(off)], dst_ref=recv.at[layer, me],
            send_sem=row_send.at[layer], recv_sem=row_recv.at[x if layer else 4],
            device_id=ahead(off), device_id_type=MESH,
        )

    drain(idrecv.at[pl.ds(0, DEVICES - 1)], id_recv)
    idcol[...] = idrecv[...].T
    row_id = lax.broadcasted_iota(jnp.int32, (SLOTS, ROWS), 1)
    for part in groups:
        one_hot = jnp.concatenate(
            [
                jnp.where(idcol[pl.ds(0, SLOTS), pl.ds(p, 1)] == row_id, 1.0, 0.0).astype(BF)
                for p in part
            ],
            axis=0,
        )
        for layer in range(2):
            rows = mm(one_hot, hist[layer]).astype(BF)
            for i, p in enumerate(part):
                mine = rows[i * SLOTS : (i + 1) * SLOTS]
                send[layer, p] = jnp.concatenate([mine[:, :128], mine[:, 128:]], axis=0)
            if layer == 0:
                for p in part:
                    row_copy(0, ORDER[p]).start()
    for off in ORDER_LATER:
        row_copy(1, off).start()

    for load in loads[3:7]:
        load.wait()
    for layer in range(2):
        wl_t[layer] = wl[layer].T
    feat_t[...] = feat[...].T

    @pl.loop(0, ROWS // TILE)
    def _(t):
        here = pl.ds(pl.multiple_of(t * TILE, TILE), TILE)
        pre = mm(feat[here, :], win[...])
        sig = jax.nn.sigmoid(pre)
        init[here, :] = (pre * sig).astype(BF)
        slope_in[here, :] = slope(pre, sig)
        adj_t[:, here] = adj[here, :].T

    fresh0 = pltpu.make_async_copy(init, fresh_h.at[0], out_sem.at[0])
    fresh0.start()

    def neighbours(state):
        @pl.loop(0, ROWS // TILE)
        def _(t):
            here = pl.ds(pl.multiple_of(t * TILE, TILE), TILE)
            base[here, :] = (1.0 - RESTART) * mm(adj[here, :], state[...]) + RESTART * init[
                here, :
            ].astype(F32)

    def columns_of(dx):
        return pl.ds(pl.multiple_of(fwd_x[-dx % 4] * (4 * SLOTS), 32 * SLOTS), 32 * SLOTS)

    def block(dx):
        return pl.ds(dx * 32 * SLOTS, 32 * SLOTS)

    def unpack(layer, dx):
        first = fwd_x[-dx % 4] * 4

        @pl.loop(0, 16)
        def _(o):
            both = [recv[layer, first + 2 * o], recv[layer, first + 2 * o + 1]]
            both = [jnp.concatenate([b[:SLOTS], b[SLOTS:]], axis=1) for b in both]
            rows = pl.ds(pl.multiple_of((dx * 16 + o) * 2 * SLOTS, 2 * SLOTS), 2 * SLOTS)
            pulled[rows, :] = jnp.concatenate(both, axis=0)

    def halo_sum(here, offsets):
        return functools.reduce(
            jnp.add, [mm(halo[here, columns_of(dx)], pulled[block(dx), :]) for dx in offsets]
        )

    neighbours(init)
    loads[7].wait()
    loads[8].wait()
    got = recv.at[0, pl.ds(0, DEVICES - 1)]
    pltpu.make_async_copy(got, got, row_recv.at[4]).wait()
    for dx in range(4):
        unpack(0, dx)

    @pl.loop(0, ROWS // TILE)
    def _(t):
        here = pl.ds(pl.multiple_of(t * TILE, TILE), TILE)
        comb = base[here, :] + (1.0 - RESTART) * halo_sum(here, range(4))
        comb_bf = comb.astype(BF)
        cb0_t[:, here] = comb_bf.T
        pre = (1.0 - MIX[0]) * comb + MIX[0] * mm(comb_bf, wl[0])
        sig = jax.nn.sigmoid(pre)
        x1[here, :] = (pre * sig).astype(BF)
        slope0[here, :] = slope(pre, sig)

    fresh1 = pltpu.make_async_copy(x1, fresh_h.at[1], out_sem.at[1])
    fresh1.start()
    neighbours(x1)

    def later(offsets):
        for dx in offsets:
            got = recv.at[1, pl.ds(0, 32 if dx else 31)]
            pltpu.make_async_copy(got, got, row_recv.at[(x - dx + 4) % 4]).wait()
        for dx in offsets:
            unpack(1, dx)

    later(EARLY)

    @pl.loop(0, ROWS // TILE)
    def _(t):
        here = pl.ds(pl.multiple_of(t * TILE, TILE), TILE)
        base[here, :] += (1.0 - RESTART) * halo_sum(here, EARLY)

    later(LATE)
    gl[...] = jnp.zeros_like(gl)

    @pl.loop(0, ROWS // TILE)
    def _(t):
        here = pl.ds(pl.multiple_of(t * TILE, TILE), TILE)
        comb = base[here, :] + (1.0 - RESTART) * halo_sum(here, LATE)
        comb_bf = comb.astype(BF)
        pre = (1.0 - MIX[1]) * comb + MIX[1] * mm(comb_bf, wl[1])
        sig = jax.nn.sigmoid(pre)
        fin[here, :] = (pre * sig).astype(BF)
        g_pre = cot[here, :] * slope(pre, sig)
        e = g_pre.astype(BF)
        gl[...] += mm(comb_bf.T, e)
        g_comb = (1.0 - MIX[1]) * g_pre + MIX[1] * mm(e, wl_t[1])
        ginit[here, :] = RESTART * g_comb
        gcb[0, here, :] = g_comb.astype(BF)

    final = pltpu.make_async_copy(fin, final_h, out_sem.at[2])
    final.start()

    seat, crew = x * 4 + z, y * 2 + core

    def share(part, to_x, to_z):
        if part < 2:
            row = part * WIDTH + (to_x * 4 + to_z) * 16
            return pl.ds(pl.multiple_of(row, 16), 16), pl.ds(0, WIDTH)
        row = 2 * WIDTH + (to_x * 2 + to_z // 2) * 16
        lane = to_z % 2 * 128
        return pl.ds(pl.multiple_of(row, 16), 16), pl.ds(pl.multiple_of(lane, 128), 128)

    def spread(part, stage, src, dst, off):
        return pltpu.make_async_remote_copy(
            src_ref=src, dst_ref=dst, send_sem=sum_send.at[part, stage],
            recv_sem=sum_recv.at[part, stage], device_id=ahead(off), device_id_type=MESH,
        )

    def lanes(part):
        return pl.ds(0, WIDTH if part < 2 else 128)

    def scatter(part, value):
        grad[pl.ds(part * WIDTH, value.shape[0]), :] = value.astype(BF)
        landing = plane_buf.at[part, seat, :, lanes(part)]
        for off in PLANE:
            rows, cols = share(part, fwd_x[off[0]] // 8, fwd_z[off[2]] // 2)
            spread(part, 0, grad.at[rows, cols], landing, off).start()
        rows, cols = share(part, x, z)
        plane_buf[part, seat, :, lanes(part)] = grad[rows, cols]

    def total(part, buf, stage):
        held = buf.at[part, pl.ds(0, buf.shape[1] - 1), :, lanes(part)]
        drain(held, sum_recv.at[part, stage])
        return jnp.sum(buf[part, :, :, lanes(part)].astype(F32), axis=0).astype(BF)

    def exchange(part):
        crew_buf[part, crew, :, lanes(part)] = total(part, plane_buf, 0)
        mine = crew_buf.at[part, crew, :, lanes(part)]
        for off in CREW:
            spread(part, 1, mine, mine, off).start()

    def gather(part):
        rows, cols = share(part, x, z)
        gsum[rows, cols] = total(part, crew_buf, 1)
        for off in PLANE:
            spread(part, 2, gsum.at[rows, cols], gsum.at[rows, cols], off).start()

    scatter(0, MIX[1] * gl[...])
    gl[...] = jnp.zeros_like(gl)

    @pl.loop(0, ROWS // TILE)
    def _(t):
        here = pl.ds(pl.multiple_of(t * TILE, TILE), TILE)
        g_state = (1.0 - RESTART) * mm(adj_t[here, :], gcb[0])
        g_pre = g_state * slope0[here, :]
        e = g_pre.astype(BF)
        gl[...] += mm(cb0_t[:, here], e)
        g_comb = (1.0 - MIX[0]) * g_pre + MIX[0] * mm(e, wl_t[0])
        ginit[here, :] += RESTART * g_comb
        gcb[1, here, :] = g_comb.astype(BF)

    scatter(1, MIX[0] * gl[...])
    exchange(0)
    gl[pl.ds(0, FIN), :] = jnp.zeros((FIN, WIDTH), F32)

    @pl.loop(0, ROWS // TILE)
    def _(t):
        here = pl.ds(pl.multiple_of(t * TILE, TILE), TILE)
        g_state = (1.0 - RESTART) * mm(adj_t[here, :], gcb[1])
        g_first = (ginit[here, :] + g_state) * slope_in[here, :]
        gl[pl.ds(0, FIN), :] += mm(feat_t[:, here], g_first.astype(BF))

    scatter(2, gl[pl.ds(0, FIN), :])
    exchange(1)
    gather(0)
    exchange(2)
    gather(1)
    gather(2)
    for part in range(3):
        for stage, buf in enumerate((plane_buf, crew_buf, plane_buf)):
            held = buf.at[part, pl.ds(0, buf.shape[1] - 1), :, lanes(part)]
            drain(held, sum_send.at[part, stage])
            if stage == 2:
                drain(held, sum_recv.at[part, stage])
    drain(idsend.at[pl.ds(0, DEVICES - 1)], id_send)
    drain(send.at[0, pl.ds(0, DEVICES - 1)], row_send.at[0])
    drain(send.at[1, pl.ds(0, DEVICES - 1)], row_send.at[1])
    fresh0.wait()
    fresh1.wait()
    final.wait()


def finish(
    fin, fresh, gsum, fin_out, fresh_out, grad_in, grad_layers,
    fin_held, fresh_held, gsum_held, first, layers, in_sem, out_sem,
):
    loads = [
        pltpu.make_async_copy(src, dst, in_sem.at[i])
        for i, (src, dst) in enumerate(
            [
                (gsum, gsum_held), (fin, fin_held), (fresh.at[0], fresh_held.at[0]),
                (fresh.at[1], fresh_held.at[1]),
            ]
        )
    ]
    stores = [
        pltpu.make_async_copy(src, dst, out_sem.at[i])
        for i, (src, dst) in enumerate(
            [
                (first, grad_in), (layers, grad_layers), (fin_held, fin_out),
                (fresh_held.at[0], fresh_out.at[0]), (fresh_held.at[1], fresh_out.at[1]),
            ]
        )
    ]
    for load in loads:
        load.start()
    factor = 1.0 / math.sqrt(ROWS * DEVICES)
    loads[0].wait()
    layers[0] = gsum_held[pl.ds(WIDTH, WIDTH), :].astype(F32) * factor
    layers[1] = gsum_held[pl.ds(0, WIDTH), :].astype(F32) * factor
    first[...] = gsum_held[pl.ds(2 * WIDTH, FIN), :].astype(F32) * factor
    stores[0].start()
    stores[1].start()
    for load, store in zip(loads[1:], stores[2:]):
        load.wait()
        store.start()
    for store in stores:
        store.wait()


def local(
    features, adjacency, halo_weights, history, pull_ids, pull_count, w_in, w_layers, cotangent
):
    anywhere = pl.BlockSpec(memory_space=pl.ANY)
    vmem = pltpu.VMEM
    dma = pltpu.SemaphoreType.DMA
    final_out, fresh, gsum = pl.pallas_call(
        kernel,
        out_shape=(
            jax.ShapeDtypeStruct((ROWS, WIDTH), BF),
            jax.ShapeDtypeStruct((2, ROWS, WIDTH), BF),
            jax.ShapeDtypeStruct((2 * WIDTH + FIN, WIDTH), BF),
        ),
        in_specs=[anywhere] * 9,
        out_specs=(anywhere, anywhere, pl.BlockSpec(memory_space=vmem)),
        scratch_shapes=[
            vmem((ROWS, FIN), BF),
            vmem((ROWS, ROWS), BF),
            vmem((ROWS, HALO), BF),
            vmem((2, ROWS, WIDTH), BF),
            vmem((SLOTS, DEVICES), jnp.int32),
            vmem((1, DEVICES), jnp.int32),
            vmem((FIN, WIDTH), BF),
            vmem((2, WIDTH, WIDTH), BF),
            vmem((ROWS, WIDTH), F32),
            vmem((DEVICES, 128), jnp.int32),
            vmem((DEVICES, 128), jnp.int32),
            vmem((128, DEVICES), jnp.int32),
            vmem((2, DEVICES, 2 * SLOTS, 128), BF),
            vmem((2, DEVICES, 2 * SLOTS, 128), BF),
            vmem((HALO, WIDTH), BF),
            vmem((ROWS, WIDTH), BF),
            vmem((ROWS, WIDTH), BF),
            vmem((ROWS, WIDTH), BF),
            vmem((ROWS, ROWS), BF),
            vmem((FIN, ROWS), BF),
            vmem((2, WIDTH, WIDTH), BF),
            vmem((WIDTH, ROWS), BF),
            vmem((ROWS, WIDTH), F32),
            vmem((ROWS, WIDTH), F32),
            vmem((ROWS, WIDTH), F32),
            vmem((ROWS, WIDTH), F32),
            vmem((2, ROWS, WIDTH), BF),
            vmem((WIDTH, WIDTH), F32),
            vmem((2 * WIDTH + FIN, WIDTH), BF),
            vmem((3, 16, 16, WIDTH), BF),
            vmem((3, 8, 16, WIDTH), BF),
            dma((9,)),
            dma((3,)),
            dma(()),
            dma(()),
            dma((2,)),
            dma((5,)),
            dma((3, 3)),
            dma((3, 3)),
        ],
        compiler_params=pltpu.CompilerParams(
            collective_id=0, has_side_effects=True, vmem_limit_bytes=VMEM_LIMIT
        ),
    )(
        features, adjacency, halo_weights, history, pull_ids.T, pull_count, w_in, w_layers, cotangent
    )
    return pl.pallas_call(
        finish,
        out_shape=(
            jax.ShapeDtypeStruct((ROWS, WIDTH), BF),
            jax.ShapeDtypeStruct((2, ROWS, WIDTH), BF),
            jax.ShapeDtypeStruct((FIN, WIDTH), F32),
            jax.ShapeDtypeStruct((2, WIDTH, WIDTH), F32),
        ),
        in_specs=[anywhere] * 3,
        out_specs=(anywhere,) * 4,
        scratch_shapes=[
            vmem((ROWS, WIDTH), BF),
            vmem((2, ROWS, WIDTH), BF),
            vmem((2 * WIDTH + FIN, WIDTH), BF),
            vmem((FIN, WIDTH), F32),
            vmem((2, WIDTH, WIDTH), F32),
            dma((4,)),
            dma((5,)),
        ],
        compiler_params=pltpu.CompilerParams(vmem_limit_bytes=VMEM_LIMIT),
    )(final_out, fresh, gsum)


def solution(mesh):
    rows = P(("dom", "rep"), None)
    history = P(None, ("dom", "rep"), None)
    return jax.shard_map(
        local,
        mesh=mesh,
        in_specs=(rows, rows, rows, history, rows, rows, P(), P(), rows),
        out_specs=(rows, history, P(), P()),
        check_vma=False,
    )
```

```python
import functools
import math
import random

import jax
import jax.numpy as jnp
from jax import lax
from jax.experimental import pallas as pl
from jax.experimental.pallas import tpu as pltpu
from jax.sharding import PartitionSpec as P

RESTART = 0.1
DECAY_RATE = 0.5
MESH = pl.DeviceIdType.MESH
BF = jnp.bfloat16
F32 = jnp.float32

ROWS = 1024
WIDTH = 256
FIN = 128
SLOTS = 24
DEVICES = 128
HALO = DEVICES * SLOTS
TILE = 1024
GROUP = 16
VMEM_LIMIT = 64 * 2**20


def shuffled(offsets, seed):
    offsets = list(offsets)
    random.Random(seed).shuffle(offsets)
    return offsets


OFFSETS = [(k // 32, k % 4, (k // 8) % 4, (k // 4) % 2) for k in range(1, DEVICES)]
ORDER = sorted(shuffled(OFFSETS, 4), key=lambda o: sum((0, 1, 2, 1)[d] for d in o[:3]))
EARLY, LATE = (1, 3), (0, 2)
ORDER_LATER = [
    o for half in (EARLY, LATE) for o in reversed(ORDER) if o[0] in half
]
PLANE = shuffled([o for o in OFFSETS if o[1] == 0 and o[3] == 0], 7)
CREW = shuffled([o for o in OFFSETS if o[0] == 0 and o[2] == 0], 8)
MIX = [math.log(DECAY_RATE / (layer + 1) + 1.0) for layer in range(2)]


def mm(a, b):
    return jnp.dot(a, b, preferred_element_type=F32)


def slope(value, sig):
    return sig * (1.0 + value * (1.0 - sig))


def kernel(
    feat_h, adj_h, halo_h, hist_h, ids_h, cnt_h, win_h, wl_h, cot_h,
    final_h, fresh_h, gsum,
    feat, adj, halo, hist, ids, cnt, win, wl, cot,
    idsend, idrecv, send, recv, pulled,
    init, x1, fin, adj_t, feat_t, wl_t, cb0_t,
    slope_in, slope0, base, ginit, gcb, gl, grad, plane_buf, crew_buf,
    in_sem, out_sem, id_send, id_recv, row_send, row_recv, sum_send, sum_recv,
):
    dom, y = lax.axis_index("dom"), lax.axis_index("rep")
    x, z, core = dom // 8, (dom // 2) % 4, dom % 2
    me = dom * 4 + y
    fwd_x = [(x + d) % 4 * 8 for d in range(4)]
    fwd_z = [(z + d) % 4 * 2 for d in range(4)]
    fwd_y = [(y + d) % 4 for d in range(4)]
    cores = [core, 1 - core]

    def ahead(off):
        return (fwd_x[off[0]] + fwd_z[off[2]] + cores[off[3]], fwd_y[off[1]])

    def behind(off):
        return (
            fwd_x[(4 - off[0]) % 4] + fwd_z[(4 - off[2]) % 4] + cores[off[3]],
            fwd_y[(4 - off[1]) % 4],
        )

    def drain(ref, sem):
        pltpu.make_async_copy(ref, ref, sem).wait()

    idrecv[pl.ds(DEVICES - 1, 1), :] = jnp.full((1, DEVICES), -1, jnp.int32)
    barrier = pltpu.get_barrier_semaphore()
    for off in ORDER:
        pl.semaphore_signal(barrier, inc=1, device_id=ahead(off), device_id_type=MESH)

    loads = [
        pltpu.make_async_copy(src, dst, in_sem.at[i])
        for i, (src, dst) in enumerate(
            [
                (ids_h, ids), (cnt_h, cnt), (hist_h, hist), (feat_h, feat), (win_h, win),
                (wl_h, wl), (adj_h, adj), (halo_h, halo), (cot_h, cot),
            ]
        )
    ]
    for load in loads:
        load.start()

    loads[0].wait()
    loads[1].wait()
    slot = lax.broadcasted_iota(jnp.int32, (SLOTS, DEVICES), 0)
    wanted = jnp.where(slot < cnt[...], ids[...], -1)
    wanted = jnp.concatenate([wanted, jnp.full((DEVICES - SLOTS, DEVICES), -1, jnp.int32)], axis=0)
    idsend[...] = wanted.T

    pl.semaphore_wait(barrier, DEVICES - 1)
    groups = [
        range(first, min(first + GROUP, DEVICES - 1)) for first in range(0, DEVICES - 1, GROUP)
    ]

    for p, off in enumerate(ORDER):
        to = behind(off)
        pltpu.make_async_remote_copy(
            src_ref=idsend.at[pl.ds(to[0] * 4 + to[1], 1)], dst_ref=idrecv.at[pl.ds(p, 1)],
            send_sem=id_send, recv_sem=id_recv.at[p // GROUP], device_id=to, device_id_type=MESH,
        ).start()
    recv[0, me] = jnp.zeros((2 * SLOTS, 128), BF)
    recv[1, me] = jnp.zeros((2 * SLOTS, 128), BF)
    loads[2].wait()

    def row_copy(layer, off):
        return pltpu.make_async_remote_copy(
            src_ref=send.at[layer, ORDER.index(off)], dst_ref=recv.at[layer, me],
            send_sem=row_send.at[layer], recv_sem=row_recv.at[x if layer else 4],
            device_id=ahead(off), device_id_type=MESH,
        )

    row_id = lax.broadcasted_iota(jnp.int32, (SLOTS, ROWS), 1)
    for g, part in enumerate(groups):
        drain(idrecv.at[pl.ds(part[0], len(part))], id_recv.at[g])
        columns = idrecv[pl.ds(g * GROUP, GROUP), :].T
        one_hot = jnp.concatenate(
            [
                jnp.where(columns[:SLOTS, i : i + 1] == row_id, 1.0, 0.0).astype(BF)
                for i in range(len(part))
            ],
            axis=0,
        )
        for layer in range(2):
            rows = mm(one_hot, hist[layer]).astype(BF)
            for i, p in enumerate(part):
                mine = rows[i * SLOTS : (i + 1) * SLOTS]
                send[layer, p] = jnp.concatenate([mine[:, :128], mine[:, 128:]], axis=0)
            if layer == 0:
                for p in part:
                    row_copy(0, ORDER[p]).start()
    for off in ORDER_LATER:
        row_copy(1, off).start()

    for load in loads[3:7]:
        load.wait()
    for layer in range(2):
        wl_t[layer] = wl[layer].T
    feat_t[...] = feat[...].T

    @pl.loop(0, ROWS // TILE)
    def _(t):
        here = pl.ds(pl.multiple_of(t * TILE, TILE), TILE)
        pre = mm(feat[here, :], win[...])
        sig = jax.nn.sigmoid(pre)
        init[here, :] = (pre * sig).astype(BF)
        slope_in[here, :] = slope(pre, sig)
        adj_t[:, here] = adj[here, :].T

    fresh0 = pltpu.make_async_copy(init, fresh_h.at[0], out_sem.at[0])
    fresh0.start()

    def neighbours(state):
        @pl.loop(0, ROWS // TILE)
        def _(t):
            here = pl.ds(pl.multiple_of(t * TILE, TILE), TILE)
            base[here, :] = (1.0 - RESTART) * mm(adj[here, :], state[...]) + RESTART * init[
                here, :
            ].astype(F32)

    def columns_of(dx):
        return pl.ds(pl.multiple_of(fwd_x[-dx % 4] * (4 * SLOTS), 32 * SLOTS), 32 * SLOTS)

    def block(dx):
        return pl.ds(dx * 32 * SLOTS, 32 * SLOTS)

    def unpack(layer, dx):
        first = fwd_x[-dx % 4] * 4

        @pl.loop(0, 16)
        def _(o):
            both = [recv[layer, first + 2 * o], recv[layer, first + 2 * o + 1]]
            both = [jnp.concatenate([b[:SLOTS], b[SLOTS:]], axis=1) for b in both]
            rows = pl.ds(pl.multiple_of((dx * 16 + o) * 2 * SLOTS, 2 * SLOTS), 2 * SLOTS)
            pulled[rows, :] = jnp.concatenate(both, axis=0)

    def halo_sum(here, offsets):
        return functools.reduce(
            jnp.add, [mm(halo[here, columns_of(dx)], pulled[block(dx), :]) for dx in offsets]
        )

    neighbours(init)
    loads[7].wait()
    loads[8].wait()
    got = recv.at[0, pl.ds(0, DEVICES - 1)]
    pltpu.make_async_copy(got, got, row_recv.at[4]).wait()
    for dx in range(4):
        unpack(0, dx)

    @pl.loop(0, ROWS // TILE)
    def _(t):
        here = pl.ds(pl.multiple_of(t * TILE, TILE), TILE)
        comb = base[here, :] + (1.0 - RESTART) * halo_sum(here, range(4))
        comb_bf = comb.astype(BF)
        cb0_t[:, here] = comb_bf.T
        pre = (1.0 - MIX[0]) * comb + MIX[0] * mm(comb_bf, wl[0])
        sig = jax.nn.sigmoid(pre)
        x1[here, :] = (pre * sig).astype(BF)
        slope0[here, :] = slope(pre, sig)

    fresh1 = pltpu.make_async_copy(x1, fresh_h.at[1], out_sem.at[1])
    fresh1.start()
    neighbours(x1)

    def later(offsets):
        for dx in offsets:
            got = recv.at[1, pl.ds(0, 32 if dx else 31)]
            pltpu.make_async_copy(got, got, row_recv.at[(x - dx + 4) % 4]).wait()
        for dx in offsets:
            unpack(1, dx)

    later(EARLY)

    @pl.loop(0, ROWS // TILE)
    def _(t):
        here = pl.ds(pl.multiple_of(t * TILE, TILE), TILE)
        base[here, :] += (1.0 - RESTART) * halo_sum(here, EARLY)

    later(LATE)
    gl[...] = jnp.zeros_like(gl)

    @pl.loop(0, ROWS // TILE)
    def _(t):
        here = pl.ds(pl.multiple_of(t * TILE, TILE), TILE)
        comb = base[here, :] + (1.0 - RESTART) * halo_sum(here, LATE)
        comb_bf = comb.astype(BF)
        pre = (1.0 - MIX[1]) * comb + MIX[1] * mm(comb_bf, wl[1])
        sig = jax.nn.sigmoid(pre)
        fin[here, :] = (pre * sig).astype(BF)
        g_pre = cot[here, :] * slope(pre, sig)
        e = g_pre.astype(BF)
        gl[...] += mm(comb_bf.T, e)
        g_comb = (1.0 - MIX[1]) * g_pre + MIX[1] * mm(e, wl_t[1])
        ginit[here, :] = RESTART * g_comb
        gcb[0, here, :] = g_comb.astype(BF)

    final = pltpu.make_async_copy(fin, final_h, out_sem.at[2])
    final.start()

    seat, crew = x * 4 + z, y * 2 + core

    def share(part, to_x, to_z):
        if part < 2:
            row = part * WIDTH + (to_x * 4 + to_z) * 16
            return pl.ds(pl.multiple_of(row, 16), 16), pl.ds(0, WIDTH)
        row = 2 * WIDTH + (to_x * 2 + to_z // 2) * 16
        lane = to_z % 2 * 128
        return pl.ds(pl.multiple_of(row, 16), 16), pl.ds(pl.multiple_of(lane, 128), 128)

    def spread(part, stage, src, dst, off):
        return pltpu.make_async_remote_copy(
            src_ref=src, dst_ref=dst, send_sem=sum_send.at[part, stage],
            recv_sem=sum_recv.at[part, stage], device_id=ahead(off), device_id_type=MESH,
        )

    def lanes(part):
        return pl.ds(0, WIDTH if part < 2 else 128)

    def scatter(part, value):
        grad[pl.ds(part * WIDTH, value.shape[0]), :] = value.astype(BF)
        landing = plane_buf.at[part, seat, :, lanes(part)]
        for off in PLANE:
            rows, cols = share(part, fwd_x[off[0]] // 8, fwd_z[off[2]] // 2)
            spread(part, 0, grad.at[rows, cols], landing, off).start()
        rows, cols = share(part, x, z)
        plane_buf[part, seat, :, lanes(part)] = grad[rows, cols]

    def total(part, buf, stage):
        held = buf.at[part, pl.ds(0, buf.shape[1] - 1), :, lanes(part)]
        drain(held, sum_recv.at[part, stage])
        return jnp.sum(buf[part, :, :, lanes(part)].astype(F32), axis=0).astype(BF)

    def exchange(part):
        crew_buf[part, crew, :, lanes(part)] = total(part, plane_buf, 0)
        mine = crew_buf.at[part, crew, :, lanes(part)]
        for off in CREW:
            spread(part, 1, mine, mine, off).start()

    def gather(part):
        rows, cols = share(part, x, z)
        gsum[rows, cols] = total(part, crew_buf, 1)
        for off in PLANE:
            spread(part, 2, gsum.at[rows, cols], gsum.at[rows, cols], off).start()

    scatter(0, MIX[1] * gl[...])
    gl[...] = jnp.zeros_like(gl)

    @pl.loop(0, ROWS // TILE)
    def _(t):
        here = pl.ds(pl.multiple_of(t * TILE, TILE), TILE)
        g_state = (1.0 - RESTART) * mm(adj_t[here, :], gcb[0])
        g_pre = g_state * slope0[here, :]
        e = g_pre.astype(BF)
        gl[...] += mm(cb0_t[:, here], e)
        g_comb = (1.0 - MIX[0]) * g_pre + MIX[0] * mm(e, wl_t[0])
        ginit[here, :] += RESTART * g_comb
        gcb[1, here, :] = g_comb.astype(BF)

    scatter(1, MIX[0] * gl[...])
    gl[pl.ds(0, FIN), :] = jnp.zeros((FIN, WIDTH), F32)

    @pl.loop(0, ROWS // TILE)
    def _(t):
        here = pl.ds(pl.multiple_of(t * TILE, TILE), TILE)
        g_state = (1.0 - RESTART) * mm(adj_t[here, :], gcb[1])
        g_first = (ginit[here, :] + g_state) * slope_in[here, :]
        gl[pl.ds(0, FIN), :] += mm(feat_t[:, here], g_first.astype(BF))

    scatter(2, gl[pl.ds(0, FIN), :])
    exchange(0)
    exchange(1)
    exchange(2)
    gather(0)
    gather(1)
    gather(2)
    for part in range(3):
        for stage, buf in enumerate((plane_buf, crew_buf, plane_buf)):
            held = buf.at[part, pl.ds(0, buf.shape[1] - 1), :, lanes(part)]
            drain(held, sum_send.at[part, stage])
            if stage == 2:
                drain(held, sum_recv.at[part, stage])
    drain(idsend.at[pl.ds(0, DEVICES - 1)], id_send)
    drain(send.at[0, pl.ds(0, DEVICES - 1)], row_send.at[0])
    drain(send.at[1, pl.ds(0, DEVICES - 1)], row_send.at[1])
    fresh0.wait()
    fresh1.wait()
    final.wait()


def finish(
    fin, fresh, gsum, fin_out, fresh_out, grad_in, grad_layers,
    fin_held, fresh_held, gsum_held, first, layers, in_sem, out_sem,
):
    loads = [
        pltpu.make_async_copy(src, dst, in_sem.at[i])
        for i, (src, dst) in enumerate(
            [
                (gsum, gsum_held), (fin, fin_held), (fresh.at[0], fresh_held.at[0]),
                (fresh.at[1], fresh_held.at[1]),
            ]
        )
    ]
    stores = [
        pltpu.make_async_copy(src, dst, out_sem.at[i])
        for i, (src, dst) in enumerate(
            [
                (first, grad_in), (layers, grad_layers), (fin_held, fin_out),
                (fresh_held.at[0], fresh_out.at[0]), (fresh_held.at[1], fresh_out.at[1]),
            ]
        )
    ]
    for load in loads:
        load.start()
    factor = 1.0 / math.sqrt(ROWS * DEVICES)
    loads[0].wait()
    layers[0] = gsum_held[pl.ds(WIDTH, WIDTH), :].astype(F32) * factor
    layers[1] = gsum_held[pl.ds(0, WIDTH), :].astype(F32) * factor
    first[...] = gsum_held[pl.ds(2 * WIDTH, FIN), :].astype(F32) * factor
    stores[0].start()
    stores[1].start()
    for load, store in zip(loads[1:], stores[2:]):
        load.wait()
        store.start()
    for store in stores:
        store.wait()


def local(
    features, adjacency, halo_weights, history, pull_ids, pull_count, w_in, w_layers, cotangent
):
    anywhere = pl.BlockSpec(memory_space=pl.ANY)
    vmem = pltpu.VMEM
    dma = pltpu.SemaphoreType.DMA
    final_out, fresh, gsum = pl.pallas_call(
        kernel,
        out_shape=(
            jax.ShapeDtypeStruct((ROWS, WIDTH), BF),
            jax.ShapeDtypeStruct((2, ROWS, WIDTH), BF),
            jax.ShapeDtypeStruct((2 * WIDTH + FIN, WIDTH), BF),
        ),
        in_specs=[anywhere] * 9,
        out_specs=(anywhere, anywhere, pl.BlockSpec(memory_space=vmem)),
        scratch_shapes=[
            vmem((ROWS, FIN), BF),
            vmem((ROWS, ROWS), BF),
            vmem((ROWS, HALO), BF),
            vmem((2, ROWS, WIDTH), BF),
            vmem((SLOTS, DEVICES), jnp.int32),
            vmem((1, DEVICES), jnp.int32),
            vmem((FIN, WIDTH), BF),
            vmem((2, WIDTH, WIDTH), BF),
            vmem((ROWS, WIDTH), F32),
            vmem((DEVICES, 128), jnp.int32),
            vmem((DEVICES, 128), jnp.int32),
            vmem((2, DEVICES, 2 * SLOTS, 128), BF),
            vmem((2, DEVICES, 2 * SLOTS, 128), BF),
            vmem((HALO, WIDTH), BF),
            vmem((ROWS, WIDTH), BF),
            vmem((ROWS, WIDTH), BF),
            vmem((ROWS, WIDTH), BF),
            vmem((ROWS, ROWS), BF),
            vmem((FIN, ROWS), BF),
            vmem((2, WIDTH, WIDTH), BF),
            vmem((WIDTH, ROWS), BF),
            vmem((ROWS, WIDTH), F32),
            vmem((ROWS, WIDTH), F32),
            vmem((ROWS, WIDTH), F32),
            vmem((ROWS, WIDTH), F32),
            vmem((2, ROWS, WIDTH), BF),
            vmem((WIDTH, WIDTH), F32),
            vmem((2 * WIDTH + FIN, WIDTH), BF),
            vmem((3, 16, 16, WIDTH), BF),
            vmem((3, 8, 16, WIDTH), BF),
            dma((9,)),
            dma((3,)),
            dma(()),
            dma((8,)),
            dma((2,)),
            dma((5,)),
            dma((3, 3)),
            dma((3, 3)),
        ],
        compiler_params=pltpu.CompilerParams(
            collective_id=0, has_side_effects=True, vmem_limit_bytes=VMEM_LIMIT
        ),
    )(
        features, adjacency, halo_weights, history, pull_ids.T, pull_count, w_in, w_layers, cotangent
    )
    return pl.pallas_call(
        finish,
        out_shape=(
            jax.ShapeDtypeStruct((ROWS, WIDTH), BF),
            jax.ShapeDtypeStruct((2, ROWS, WIDTH), BF),
            jax.ShapeDtypeStruct((FIN, WIDTH), F32),
            jax.ShapeDtypeStruct((2, WIDTH, WIDTH), F32),
        ),
        in_specs=[anywhere] * 3,
        out_specs=(anywhere,) * 4,
        scratch_shapes=[
            vmem((ROWS, WIDTH), BF),
            vmem((2, ROWS, WIDTH), BF),
            vmem((2 * WIDTH + FIN, WIDTH), BF),
            vmem((FIN, WIDTH), F32),
            vmem((2, WIDTH, WIDTH), F32),
            dma((4,)),
            dma((5,)),
        ],
        compiler_params=pltpu.CompilerParams(vmem_limit_bytes=VMEM_LIMIT),
    )(final_out, fresh, gsum)


def solution(mesh):
    rows = P(("dom", "rep"), None)
    history = P(None, ("dom", "rep"), None)
    return jax.shard_map(
        local,
        mesh=mesh,
        in_specs=(rows, rows, rows, history, rows, rows, P(), P(), rows),
        out_specs=(rows, history, P(), P()),
        check_vma=False,
    )
```

```python
import functools
import math
import random

import jax
import jax.numpy as jnp
from jax import lax
from jax.experimental import pallas as pl
from jax.experimental.pallas import tpu as pltpu
from jax.sharding import PartitionSpec as P

RESTART = 0.1
DECAY_RATE = 0.5
MESH = pl.DeviceIdType.MESH
BF = jnp.bfloat16
F32 = jnp.float32

ROWS = 1024
WIDTH = 256
FIN = 128
SLOTS = 24
DEVICES = 128
HALO = DEVICES * SLOTS
TILE = 1024
GROUP = 16
VMEM_LIMIT = 64 * 2**20


def shuffled(offsets, seed):
    offsets = list(offsets)
    random.Random(seed).shuffle(offsets)
    return offsets


OFFSETS = [(k // 32, k % 4, (k // 8) % 4, (k // 4) % 2) for k in range(1, DEVICES)]
def hops(off):
    return sum((0, 1, 2, 1)[d] for d in off[:3])


NEAREST = sorted(shuffled(OFFSETS, 4), key=hops)
ORDER = NEAREST[:48] + shuffled(NEAREST[48:], 5)
EARLY, LATE = (1, 3), (0, 2)
ORDER_LATER = [o for half in (EARLY, LATE) for o in reversed(NEAREST) if o[0] in half]
PLANE = shuffled([o for o in OFFSETS if o[1] == 0 and o[3] == 0], 7)
CREW = shuffled([o for o in OFFSETS if o[0] == 0 and o[2] == 0], 8)
MIX = [math.log(DECAY_RATE / (layer + 1) + 1.0) for layer in range(2)]


def mm(a, b):
    return jnp.dot(a, b, preferred_element_type=F32)


def slope(value, sig):
    return sig * (1.0 + value * (1.0 - sig))


def kernel(
    feat_h, adj_h, halo_h, hist_h, ids_h, cnt_h, win_h, wl_h, cot_h,
    final_h, fresh_h, gsum,
    feat, adj, halo, hist, ids, cnt, win, wl, cot,
    idsend, idrecv, one_hot, send, recv, pulled,
    init, x1, fin, adj_t, feat_t, wl_t, cb0_t,
    slope_in, slope0, base, ginit, gcb, gl, grad, plane_buf, crew_buf,
    in_sem, out_sem, id_send, id_recv, row_send, row_recv, sum_send, sum_recv,
):
    dom, y = lax.axis_index("dom"), lax.axis_index("rep")
    x, z, core = dom // 8, (dom // 2) % 4, dom % 2
    me = dom * 4 + y
    fwd_x = [(x + d) % 4 * 8 for d in range(4)]
    fwd_z = [(z + d) % 4 * 2 for d in range(4)]
    fwd_y = [(y + d) % 4 for d in range(4)]
    cores = [core, 1 - core]

    def ahead(off):
        return (fwd_x[off[0]] + fwd_z[off[2]] + cores[off[3]], fwd_y[off[1]])

    def behind(off):
        return (
            fwd_x[(4 - off[0]) % 4] + fwd_z[(4 - off[2]) % 4] + cores[off[3]],
            fwd_y[(4 - off[1]) % 4],
        )

    def drain(ref, sem):
        pltpu.make_async_copy(ref, ref, sem).wait()

    idrecv[pl.ds(DEVICES - 1, 1), :] = jnp.full((1, DEVICES), -1, jnp.int32)
    barrier = pltpu.get_barrier_semaphore()
    for off in reversed(NEAREST):
        pl.semaphore_signal(barrier, inc=1, device_id=ahead(off), device_id_type=MESH)

    loads = [
        pltpu.make_async_copy(src, dst, in_sem.at[i])
        for i, (src, dst) in enumerate(
            [
                (ids_h, ids), (cnt_h, cnt), (hist_h, hist), (feat_h, feat), (win_h, win),
                (wl_h, wl), (adj_h, adj), (halo_h, halo), (cot_h, cot),
            ]
        )
    ]
    for load in loads:
        load.start()

    loads[0].wait()
    loads[1].wait()
    slot = lax.broadcasted_iota(jnp.int32, (SLOTS, DEVICES), 0)
    wanted = jnp.where(slot < cnt[...], ids[...], -1)
    wanted = jnp.concatenate([wanted, jnp.full((DEVICES - SLOTS, DEVICES), -1, jnp.int32)], axis=0)
    idsend[...] = wanted.T

    pl.semaphore_wait(barrier, DEVICES - 1)
    groups = [
        range(first, min(first + GROUP, DEVICES - 1)) for first in range(0, DEVICES - 1, GROUP)
    ]

    for p, off in enumerate(ORDER):
        to = behind(off)
        pltpu.make_async_remote_copy(
            src_ref=idsend.at[pl.ds(to[0] * 4 + to[1], 1)], dst_ref=idrecv.at[pl.ds(p, 1)],
            send_sem=id_send, recv_sem=id_recv.at[p // GROUP], device_id=to, device_id_type=MESH,
        ).start()
    recv[0, me] = jnp.zeros((2 * SLOTS, 128), BF)
    recv[1, me] = jnp.zeros((2 * SLOTS, 128), BF)
    loads[2].wait()

    def row_copy(layer, off):
        return pltpu.make_async_remote_copy(
            src_ref=send.at[layer, ORDER.index(off)], dst_ref=recv.at[layer, me],
            send_sem=row_send.at[layer], recv_sem=row_recv.at[x if layer else 4],
            device_id=ahead(off), device_id_type=MESH,
        )

    def pick(layer, g, part):
        rows = mm(one_hot[g, pl.ds(0, len(part) * SLOTS), :], hist[layer]).astype(BF)
        for i, p in enumerate(part):
            mine = rows[i * SLOTS : (i + 1) * SLOTS]
            send[layer, p] = jnp.concatenate([mine[:, :128], mine[:, 128:]], axis=0)

    row_id = lax.broadcasted_iota(jnp.int32, (SLOTS, ROWS), 1)
    for g, part in enumerate(groups):
        drain(idrecv.at[pl.ds(part[0], len(part))], id_recv.at[g])
        columns = idrecv[pl.ds(g * GROUP, GROUP), :].T
        one_hot[g, pl.ds(0, len(part) * SLOTS), :] = jnp.concatenate(
            [
                jnp.where(columns[:SLOTS, i : i + 1] == row_id, 1.0, 0.0).astype(BF)
                for i in range(len(part))
            ],
            axis=0,
        )
        pick(0, g, part)
        for p in part:
            row_copy(0, ORDER[p]).start()
    for g, part in enumerate(groups):
        pick(1, g, part)
    for off in ORDER_LATER:
        row_copy(1, off).start()

    for load in loads[3:7]:
        load.wait()
    for layer in range(2):
        wl_t[layer] = wl[layer].T
    feat_t[...] = feat[...].T

    @pl.loop(0, ROWS // TILE)
    def _(t):
        here = pl.ds(pl.multiple_of(t * TILE, TILE), TILE)
        pre = mm(feat[here, :], win[...])
        sig = jax.nn.sigmoid(pre)
        init[here, :] = (pre * sig).astype(BF)
        slope_in[here, :] = slope(pre, sig)
        adj_t[:, here] = adj[here, :].T

    fresh0 = pltpu.make_async_copy(init, fresh_h.at[0], out_sem.at[0])
    fresh0.start()

    def neighbours(state):
        @pl.loop(0, ROWS // TILE)
        def _(t):
            here = pl.ds(pl.multiple_of(t * TILE, TILE), TILE)
            base[here, :] = (1.0 - RESTART) * mm(adj[here, :], state[...]) + RESTART * init[
                here, :
            ].astype(F32)

    def columns_of(dx):
        return pl.ds(pl.multiple_of(fwd_x[-dx % 4] * (4 * SLOTS), 32 * SLOTS), 32 * SLOTS)

    def block(dx):
        return pl.ds(dx * 32 * SLOTS, 32 * SLOTS)

    def unpack(layer, dx):
        first = fwd_x[-dx % 4] * 4

        @pl.loop(0, 16)
        def _(o):
            both = [recv[layer, first + 2 * o], recv[layer, first + 2 * o + 1]]
            both = [jnp.concatenate([b[:SLOTS], b[SLOTS:]], axis=1) for b in both]
            rows = pl.ds(pl.multiple_of((dx * 16 + o) * 2 * SLOTS, 2 * SLOTS), 2 * SLOTS)
            pulled[rows, :] = jnp.concatenate(both, axis=0)

    def halo_sum(here, offsets):
        return functools.reduce(
            jnp.add, [mm(halo[here, columns_of(dx)], pulled[block(dx), :]) for dx in offsets]
        )

    neighbours(init)
    loads[7].wait()
    loads[8].wait()
    got = recv.at[0, pl.ds(0, DEVICES - 1)]
    pltpu.make_async_copy(got, got, row_recv.at[4]).wait()
    for dx in range(4):
        unpack(0, dx)

    @pl.loop(0, ROWS // TILE)
    def _(t):
        here = pl.ds(pl.multiple_of(t * TILE, TILE), TILE)
        comb = base[here, :] + (1.0 - RESTART) * halo_sum(here, range(4))
        comb_bf = comb.astype(BF)
        cb0_t[:, here] = comb_bf.T
        pre = (1.0 - MIX[0]) * comb + MIX[0] * mm(comb_bf, wl[0])
        sig = jax.nn.sigmoid(pre)
        x1[here, :] = (pre * sig).astype(BF)
        slope0[here, :] = slope(pre, sig)

    fresh1 = pltpu.make_async_copy(x1, fresh_h.at[1], out_sem.at[1])
    fresh1.start()
    neighbours(x1)

    def later(offsets):
        for dx in offsets:
            got = recv.at[1, pl.ds(0, 32 if dx else 31)]
            pltpu.make_async_copy(got, got, row_recv.at[(x - dx + 4) % 4]).wait()
        for dx in offsets:
            unpack(1, dx)

    later(EARLY)

    @pl.loop(0, ROWS // TILE)
    def _(t):
        here = pl.ds(pl.multiple_of(t * TILE, TILE), TILE)
        base[here, :] += (1.0 - RESTART) * halo_sum(here, EARLY)

    later(LATE)
    gl[...] = jnp.zeros_like(gl)

    @pl.loop(0, ROWS // TILE)
    def _(t):
        here = pl.ds(pl.multiple_of(t * TILE, TILE), TILE)
        comb = base[here, :] + (1.0 - RESTART) * halo_sum(here, LATE)
        comb_bf = comb.astype(BF)
        pre = (1.0 - MIX[1]) * comb + MIX[1] * mm(comb_bf, wl[1])
        sig = jax.nn.sigmoid(pre)
        fin[here, :] = (pre * sig).astype(BF)
        g_pre = cot[here, :] * slope(pre, sig)
        e = g_pre.astype(BF)
        gl[...] += mm(comb_bf.T, e)
        g_comb = (1.0 - MIX[1]) * g_pre + MIX[1] * mm(e, wl_t[1])
        ginit[here, :] = RESTART * g_comb
        gcb[0, here, :] = g_comb.astype(BF)

    final = pltpu.make_async_copy(fin, final_h, out_sem.at[2])
    final.start()

    seat, crew = x * 4 + z, y * 2 + core

    def share(part, to_x, to_z):
        if part < 2:
            row = part * WIDTH + (to_x * 4 + to_z) * 16
            return pl.ds(pl.multiple_of(row, 16), 16), pl.ds(0, WIDTH)
        row = 2 * WIDTH + (to_x * 2 + to_z // 2) * 16
        lane = to_z % 2 * 128
        return pl.ds(pl.multiple_of(row, 16), 16), pl.ds(pl.multiple_of(lane, 128), 128)

    def spread(part, stage, src, dst, off):
        return pltpu.make_async_remote_copy(
            src_ref=src, dst_ref=dst, send_sem=sum_send.at[part, stage],
            recv_sem=sum_recv.at[part, stage], device_id=ahead(off), device_id_type=MESH,
        )

    def lanes(part):
        return pl.ds(0, WIDTH if part < 2 else 128)

    def scatter(part, value):
        grad[pl.ds(part * WIDTH, value.shape[0]), :] = value.astype(BF)
        landing = plane_buf.at[part, seat, :, lanes(part)]
        for off in PLANE:
            rows, cols = share(part, fwd_x[off[0]] // 8, fwd_z[off[2]] // 2)
            spread(part, 0, grad.at[rows, cols], landing, off).start()
        rows, cols = share(part, x, z)
        plane_buf[part, seat, :, lanes(part)] = grad[rows, cols]

    def total(part, buf, stage):
        held = buf.at[part, pl.ds(0, buf.shape[1] - 1), :, lanes(part)]
        drain(held, sum_recv.at[part, stage])
        return jnp.sum(buf[part, :, :, lanes(part)].astype(F32), axis=0).astype(BF)

    def exchange(part):
        crew_buf[part, crew, :, lanes(part)] = total(part, plane_buf, 0)
        mine = crew_buf.at[part, crew, :, lanes(part)]
        for off in CREW:
            spread(part, 1, mine, mine, off).start()

    def gather(part):
        rows, cols = share(part, x, z)
        gsum[rows, cols] = total(part, crew_buf, 1)
        for off in PLANE:
            spread(part, 2, gsum.at[rows, cols], gsum.at[rows, cols], off).start()

    scatter(0, MIX[1] * gl[...])
    gl[...] = jnp.zeros_like(gl)

    @pl.loop(0, ROWS // TILE)
    def _(t):
        here = pl.ds(pl.multiple_of(t * TILE, TILE), TILE)
        g_state = (1.0 - RESTART) * mm(adj_t[here, :], gcb[0])
        g_pre = g_state * slope0[here, :]
        e = g_pre.astype(BF)
        gl[...] += mm(cb0_t[:, here], e)
        g_comb = (1.0 - MIX[0]) * g_pre + MIX[0] * mm(e, wl_t[0])
        ginit[here, :] += RESTART * g_comb
        gcb[1, here, :] = g_comb.astype(BF)

    scatter(1, MIX[0] * gl[...])
    gl[pl.ds(0, FIN), :] = jnp.zeros((FIN, WIDTH), F32)

    @pl.loop(0, ROWS // TILE)
    def _(t):
        here = pl.ds(pl.multiple_of(t * TILE, TILE), TILE)
        g_state = (1.0 - RESTART) * mm(adj_t[here, :], gcb[1])
        g_first = (ginit[here, :] + g_state) * slope_in[here, :]
        gl[pl.ds(0, FIN), :] += mm(feat_t[:, here], g_first.astype(BF))

    scatter(2, gl[pl.ds(0, FIN), :])
    exchange(0)
    exchange(1)
    exchange(2)
    gather(0)
    gather(1)
    gather(2)
    for part in range(3):
        for stage, buf in enumerate((plane_buf, crew_buf, plane_buf)):
            held = buf.at[part, pl.ds(0, buf.shape[1] - 1), :, lanes(part)]
            drain(held, sum_send.at[part, stage])
            if stage == 2:
                drain(held, sum_recv.at[part, stage])
    drain(idsend.at[pl.ds(0, DEVICES - 1)], id_send)
    drain(send.at[0, pl.ds(0, DEVICES - 1)], row_send.at[0])
    drain(send.at[1, pl.ds(0, DEVICES - 1)], row_send.at[1])
    fresh0.wait()
    fresh1.wait()
    final.wait()


def finish(
    fin, fresh, gsum, fin_out, fresh_out, grad_in, grad_layers,
    fin_held, fresh_held, gsum_held, first, layers, in_sem, out_sem,
):
    loads = [
        pltpu.make_async_copy(src, dst, in_sem.at[i])
        for i, (src, dst) in enumerate(
            [
                (gsum, gsum_held), (fin, fin_held), (fresh.at[0], fresh_held.at[0]),
                (fresh.at[1], fresh_held.at[1]),
            ]
        )
    ]
    stores = [
        pltpu.make_async_copy(src, dst, out_sem.at[i])
        for i, (src, dst) in enumerate(
            [
                (first, grad_in), (layers, grad_layers), (fin_held, fin_out),
                (fresh_held.at[0], fresh_out.at[0]), (fresh_held.at[1], fresh_out.at[1]),
            ]
        )
    ]
    for load in loads:
        load.start()
    factor = 1.0 / math.sqrt(ROWS * DEVICES)
    loads[0].wait()
    layers[0] = gsum_held[pl.ds(WIDTH, WIDTH), :].astype(F32) * factor
    layers[1] = gsum_held[pl.ds(0, WIDTH), :].astype(F32) * factor
    first[...] = gsum_held[pl.ds(2 * WIDTH, FIN), :].astype(F32) * factor
    stores[0].start()
    stores[1].start()
    for load, store in zip(loads[1:], stores[2:]):
        load.wait()
        store.start()
    for store in stores:
        store.wait()


def local(
    features, adjacency, halo_weights, history, pull_ids, pull_count, w_in, w_layers, cotangent
):
    anywhere = pl.BlockSpec(memory_space=pl.ANY)
    vmem = pltpu.VMEM
    dma = pltpu.SemaphoreType.DMA
    final_out, fresh, gsum = pl.pallas_call(
        kernel,
        out_shape=(
            jax.ShapeDtypeStruct((ROWS, WIDTH), BF),
            jax.ShapeDtypeStruct((2, ROWS, WIDTH), BF),
            jax.ShapeDtypeStruct((2 * WIDTH + FIN, WIDTH), BF),
        ),
        in_specs=[anywhere] * 9,
        out_specs=(anywhere, anywhere, pl.BlockSpec(memory_space=vmem)),
        scratch_shapes=[
            vmem((ROWS, FIN), BF),
            vmem((ROWS, ROWS), BF),
            vmem((ROWS, HALO), BF),
            vmem((2, ROWS, WIDTH), BF),
            vmem((SLOTS, DEVICES), jnp.int32),
            vmem((1, DEVICES), jnp.int32),
            vmem((FIN, WIDTH), BF),
            vmem((2, WIDTH, WIDTH), BF),
            vmem((ROWS, WIDTH), F32),
            vmem((DEVICES, 128), jnp.int32),
            vmem((DEVICES, 128), jnp.int32),
            vmem((DEVICES // GROUP, GROUP * SLOTS, ROWS), BF),
            vmem((2, DEVICES, 2 * SLOTS, 128), BF),
            vmem((2, DEVICES, 2 * SLOTS, 128), BF),
            vmem((HALO, WIDTH), BF),
            vmem((ROWS, WIDTH), BF),
            vmem((ROWS, WIDTH), BF),
            vmem((ROWS, WIDTH), BF),
            vmem((ROWS, ROWS), BF),
            vmem((FIN, ROWS), BF),
            vmem((2, WIDTH, WIDTH), BF),
            vmem((WIDTH, ROWS), BF),
            vmem((ROWS, WIDTH), F32),
            vmem((ROWS, WIDTH), F32),
            vmem((ROWS, WIDTH), F32),
            vmem((ROWS, WIDTH), F32),
            vmem((2, ROWS, WIDTH), BF),
            vmem((WIDTH, WIDTH), F32),
            vmem((2 * WIDTH + FIN, WIDTH), BF),
            vmem((3, 16, 16, WIDTH), BF),
            vmem((3, 8, 16, WIDTH), BF),
            dma((9,)),
            dma((3,)),
            dma(()),
            dma((8,)),
            dma((2,)),
            dma((5,)),
            dma((3, 3)),
            dma((3, 3)),
        ],
        compiler_params=pltpu.CompilerParams(
            collective_id=0, has_side_effects=True, vmem_limit_bytes=VMEM_LIMIT
        ),
    )(
        features, adjacency, halo_weights, history, pull_ids.T, pull_count, w_in, w_layers, cotangent
    )
    return pl.pallas_call(
        finish,
        out_shape=(
            jax.ShapeDtypeStruct((ROWS, WIDTH), BF),
            jax.ShapeDtypeStruct((2, ROWS, WIDTH), BF),
            jax.ShapeDtypeStruct((FIN, WIDTH), F32),
            jax.ShapeDtypeStruct((2, WIDTH, WIDTH), F32),
        ),
        in_specs=[anywhere] * 3,
        out_specs=(anywhere,) * 4,
        scratch_shapes=[
            vmem((ROWS, WIDTH), BF),
            vmem((2, ROWS, WIDTH), BF),
            vmem((2 * WIDTH + FIN, WIDTH), BF),
            vmem((FIN, WIDTH), F32),
            vmem((2, WIDTH, WIDTH), F32),
            dma((4,)),
            dma((5,)),
        ],
        compiler_params=pltpu.CompilerParams(vmem_limit_bytes=VMEM_LIMIT),
    )(final_out, fresh, gsum)


def solution(mesh):
    rows = P(("dom", "rep"), None)
    history = P(None, ("dom", "rep"), None)
    return jax.shard_map(
        local,
        mesh=mesh,
        in_specs=(rows, rows, rows, history, rows, rows, P(), P(), rows),
        out_specs=(rows, history, P(), P()),
        check_vma=False,
    )
```

```python
import functools
import math
import random

import jax
import jax.numpy as jnp
from jax import lax
from jax.experimental import pallas as pl
from jax.experimental.pallas import tpu as pltpu
from jax.sharding import PartitionSpec as P

RESTART = 0.1
DECAY_RATE = 0.5
MESH = pl.DeviceIdType.MESH
BF = jnp.bfloat16
F32 = jnp.float32

ROWS = 1024
WIDTH = 256
FIN = 128
SLOTS = 24
DEVICES = 128
HALO = DEVICES * SLOTS
TILE = 1024
GROUP = 16
VMEM_LIMIT = 64 * 2**20


def shuffled(offsets, seed):
    offsets = list(offsets)
    random.Random(seed).shuffle(offsets)
    return offsets


OFFSETS = [(k // 32, k % 4, (k // 8) % 4, (k // 4) % 2) for k in range(1, DEVICES)]
def hops(off):
    return sum((0, 1, 2, 1)[d] for d in off[:3])


NEAREST = sorted(shuffled(OFFSETS, 4), key=hops)
ORDER = NEAREST[:48] + shuffled(NEAREST[48:], 5)
EARLY, LATE = (1, 3), (0, 2)
ORDER_LATER = [o for half in (EARLY, LATE) for o in reversed(NEAREST) if o[0] in half]
PLANE = [o for o in reversed(NEAREST) if o[1] == 0 and o[3] == 0]
CREW = [o for o in reversed(NEAREST) if o[0] == 0 and o[2] == 0]
MIX = [math.log(DECAY_RATE / (layer + 1) + 1.0) for layer in range(2)]


def mm(a, b):
    return jnp.dot(a, b, preferred_element_type=F32)


def slope(value, sig):
    return sig * (1.0 + value * (1.0 - sig))


def kernel(
    feat_h, adj_h, halo_h, hist_h, ids_h, cnt_h, win_h, wl_h, cot_h,
    final_h, fresh_h, gsum,
    feat, adj, halo, hist, ids, cnt, win, wl, cot,
    idsend, idrecv, one_hot, send, recv, pulled,
    init, x1, fin, adj_t, feat_t, wl_t, cb0_t,
    slope_in, slope0, base, ginit, gcb, gl, grad, plane_buf, crew_buf,
    in_sem, out_sem, id_send, id_recv, row_send, row_recv, sum_send, sum_recv,
):
    dom, y = lax.axis_index("dom"), lax.axis_index("rep")
    x, z, core = dom // 8, (dom // 2) % 4, dom % 2
    me = dom * 4 + y
    fwd_x = [(x + d) % 4 * 8 for d in range(4)]
    fwd_z = [(z + d) % 4 * 2 for d in range(4)]
    fwd_y = [(y + d) % 4 for d in range(4)]
    cores = [core, 1 - core]

    def ahead(off):
        return (fwd_x[off[0]] + fwd_z[off[2]] + cores[off[3]], fwd_y[off[1]])

    def behind(off):
        return (
            fwd_x[(4 - off[0]) % 4] + fwd_z[(4 - off[2]) % 4] + cores[off[3]],
            fwd_y[(4 - off[1]) % 4],
        )

    def drain(ref, sem):
        pltpu.make_async_copy(ref, ref, sem).wait()

    idrecv[pl.ds(DEVICES - 1, 1), :] = jnp.full((1, DEVICES), -1, jnp.int32)
    barrier = pltpu.get_barrier_semaphore()
    for off in reversed(NEAREST):
        pl.semaphore_signal(barrier, inc=1, device_id=ahead(off), device_id_type=MESH)

    loads = [
        pltpu.make_async_copy(src, dst, in_sem.at[i])
        for i, (src, dst) in enumerate(
            [
                (ids_h, ids), (cnt_h, cnt), (hist_h, hist), (feat_h, feat), (win_h, win),
                (wl_h, wl), (adj_h, adj), (halo_h, halo), (cot_h, cot),
            ]
        )
    ]
    for load in loads:
        load.start()

    loads[0].wait()
    loads[1].wait()
    slot = lax.broadcasted_iota(jnp.int32, (SLOTS, DEVICES), 0)
    wanted = jnp.where(slot < cnt[...], ids[...], -1)
    wanted = jnp.concatenate([wanted, jnp.full((DEVICES - SLOTS, DEVICES), -1, jnp.int32)], axis=0)
    idsend[...] = wanted.T

    pl.semaphore_wait(barrier, DEVICES - 1)
    groups = [
        range(first, min(first + GROUP, DEVICES - 1)) for first in range(0, DEVICES - 1, GROUP)
    ]

    for p, off in enumerate(ORDER):
        to = behind(off)
        pltpu.make_async_remote_copy(
            src_ref=idsend.at[pl.ds(to[0] * 4 + to[1], 1)], dst_ref=idrecv.at[pl.ds(p, 1)],
            send_sem=id_send, recv_sem=id_recv.at[p // GROUP], device_id=to, device_id_type=MESH,
        ).start()
    recv[0, me] = jnp.zeros((2 * SLOTS, 128), BF)
    recv[1, me] = jnp.zeros((2 * SLOTS, 128), BF)
    loads[2].wait()

    def row_copy(layer, off):
        return pltpu.make_async_remote_copy(
            src_ref=send.at[layer, ORDER.index(off)], dst_ref=recv.at[layer, me],
            send_sem=row_send.at[layer], recv_sem=row_recv.at[x if layer else 4],
            device_id=ahead(off), device_id_type=MESH,
        )

    def pick(layer, g, part):
        rows = mm(one_hot[g, pl.ds(0, len(part) * SLOTS), :], hist[layer]).astype(BF)
        for i, p in enumerate(part):
            mine = rows[i * SLOTS : (i + 1) * SLOTS]
            send[layer, p] = jnp.concatenate([mine[:, :128], mine[:, 128:]], axis=0)

    row_id = lax.broadcasted_iota(jnp.int32, (SLOTS, ROWS), 1)
    for g, part in enumerate(groups):
        drain(idrecv.at[pl.ds(part[0], len(part))], id_recv.at[g])
        columns = idrecv[pl.ds(g * GROUP, GROUP), :].T
        one_hot[g, pl.ds(0, len(part) * SLOTS), :] = jnp.concatenate(
            [
                jnp.where(columns[:SLOTS, i : i + 1] == row_id, 1.0, 0.0).astype(BF)
                for i in range(len(part))
            ],
            axis=0,
        )
        pick(0, g, part)
        for p in part:
            row_copy(0, ORDER[p]).start()
    for g, part in enumerate(groups):
        pick(1, g, part)
    for off in ORDER_LATER:
        row_copy(1, off).start()

    for load in loads[3:7]:
        load.wait()
    for layer in range(2):
        wl_t[layer] = wl[layer].T
    feat_t[...] = feat[...].T

    @pl.loop(0, ROWS // TILE)
    def _(t):
        here = pl.ds(pl.multiple_of(t * TILE, TILE), TILE)
        pre = mm(feat[here, :], win[...])
        sig = jax.nn.sigmoid(pre)
        init[here, :] = (pre * sig).astype(BF)
        slope_in[here, :] = slope(pre, sig)
        adj_t[:, here] = adj[here, :].T

    fresh0 = pltpu.make_async_copy(init, fresh_h.at[0], out_sem.at[0])
    fresh0.start()

    def neighbours(state):
        @pl.loop(0, ROWS // TILE)
        def _(t):
            here = pl.ds(pl.multiple_of(t * TILE, TILE), TILE)
            base[here, :] = (1.0 - RESTART) * mm(adj[here, :], state[...]) + RESTART * init[
                here, :
            ].astype(F32)

    def columns_of(dx):
        return pl.ds(pl.multiple_of(fwd_x[-dx % 4] * (4 * SLOTS), 32 * SLOTS), 32 * SLOTS)

    def block(dx):
        return pl.ds(dx * 32 * SLOTS, 32 * SLOTS)

    def unpack(layer, dx):
        first = fwd_x[-dx % 4] * 4

        @pl.loop(0, 16)
        def _(o):
            both = [recv[layer, first + 2 * o], recv[layer, first + 2 * o + 1]]
            both = [jnp.concatenate([b[:SLOTS], b[SLOTS:]], axis=1) for b in both]
            rows = pl.ds(pl.multiple_of((dx * 16 + o) * 2 * SLOTS, 2 * SLOTS), 2 * SLOTS)
            pulled[rows, :] = jnp.concatenate(both, axis=0)

    def halo_sum(here, offsets):
        return functools.reduce(
            jnp.add, [mm(halo[here, columns_of(dx)], pulled[block(dx), :]) for dx in offsets]
        )

    neighbours(init)
    loads[7].wait()
    loads[8].wait()
    got = recv.at[0, pl.ds(0, DEVICES - 1)]
    pltpu.make_async_copy(got, got, row_recv.at[4]).wait()
    for dx in range(4):
        unpack(0, dx)

    @pl.loop(0, ROWS // TILE)
    def _(t):
        here = pl.ds(pl.multiple_of(t * TILE, TILE), TILE)
        comb = base[here, :] + (1.0 - RESTART) * halo_sum(here, range(4))
        comb_bf = comb.astype(BF)
        cb0_t[:, here] = comb_bf.T
        pre = (1.0 - MIX[0]) * comb + MIX[0] * mm(comb_bf, wl[0])
        sig = jax.nn.sigmoid(pre)
        x1[here, :] = (pre * sig).astype(BF)
        slope0[here, :] = slope(pre, sig)

    fresh1 = pltpu.make_async_copy(x1, fresh_h.at[1], out_sem.at[1])
    fresh1.start()
    neighbours(x1)

    def later(offsets):
        for dx in offsets:
            got = recv.at[1, pl.ds(0, 32 if dx else 31)]
            pltpu.make_async_copy(got, got, row_recv.at[(x - dx + 4) % 4]).wait()
        for dx in offsets:
            unpack(1, dx)

    later(EARLY)

    @pl.loop(0, ROWS // TILE)
    def _(t):
        here = pl.ds(pl.multiple_of(t * TILE, TILE), TILE)
        base[here, :] += (1.0 - RESTART) * halo_sum(here, EARLY)

    later(LATE)
    gl[...] = jnp.zeros_like(gl)

    @pl.loop(0, ROWS // TILE)
    def _(t):
        here = pl.ds(pl.multiple_of(t * TILE, TILE), TILE)
        comb = base[here, :] + (1.0 - RESTART) * halo_sum(here, LATE)
        comb_bf = comb.astype(BF)
        pre = (1.0 - MIX[1]) * comb + MIX[1] * mm(comb_bf, wl[1])
        sig = jax.nn.sigmoid(pre)
        fin[here, :] = (pre * sig).astype(BF)
        g_pre = cot[here, :] * slope(pre, sig)
        e = g_pre.astype(BF)
        gl[...] += mm(comb_bf.T, e)
        g_comb = (1.0 - MIX[1]) * g_pre + MIX[1] * mm(e, wl_t[1])
        ginit[here, :] = RESTART * g_comb
        gcb[0, here, :] = g_comb.astype(BF)

    final = pltpu.make_async_copy(fin, final_h, out_sem.at[2])
    final.start()

    seat, crew = x * 4 + z, y * 2 + core

    def share(part, to_x, to_z):
        if part < 2:
            row = part * WIDTH + (to_x * 4 + to_z) * 16
            return pl.ds(pl.multiple_of(row, 16), 16), pl.ds(0, WIDTH)
        row = 2 * WIDTH + (to_x * 2 + to_z // 2) * 16
        lane = to_z % 2 * 128
        return pl.ds(pl.multiple_of(row, 16), 16), pl.ds(pl.multiple_of(lane, 128), 128)

    def spread(part, stage, src, dst, off):
        return pltpu.make_async_remote_copy(
            src_ref=src, dst_ref=dst, send_sem=sum_send.at[part, stage],
            recv_sem=sum_recv.at[part, stage], device_id=ahead(off), device_id_type=MESH,
        )

    def lanes(part):
        return pl.ds(0, WIDTH if part < 2 else 128)

    def scatter(part, value):
        grad[pl.ds(part * WIDTH, value.shape[0]), :] = value.astype(BF)
        landing = plane_buf.at[part, seat, :, lanes(part)]
        for off in PLANE:
            rows, cols = share(part, fwd_x[off[0]] // 8, fwd_z[off[2]] // 2)
            spread(part, 0, grad.at[rows, cols], landing, off).start()
        rows, cols = share(part, x, z)
        plane_buf[part, seat, :, lanes(part)] = grad[rows, cols]

    def total(part, buf, stage):
        held = buf.at[part, pl.ds(0, buf.shape[1] - 1), :, lanes(part)]
        drain(held, sum_recv.at[part, stage])
        return jnp.sum(buf[part, :, :, lanes(part)].astype(F32), axis=0).astype(BF)

    def exchange(part):
        crew_buf[part, crew, :, lanes(part)] = total(part, plane_buf, 0)
        mine = crew_buf.at[part, crew, :, lanes(part)]
        for off in CREW:
            spread(part, 1, mine, mine, off).start()

    def gather(part):
        rows, cols = share(part, x, z)
        gsum[rows, cols] = total(part, crew_buf, 1)
        for off in PLANE:
            spread(part, 2, gsum.at[rows, cols], gsum.at[rows, cols], off).start()

    scatter(0, MIX[1] * gl[...])
    gl[...] = jnp.zeros_like(gl)

    @pl.loop(0, ROWS // TILE)
    def _(t):
        here = pl.ds(pl.multiple_of(t * TILE, TILE), TILE)
        g_state = (1.0 - RESTART) * mm(adj_t[here, :], gcb[0])
        g_pre = g_state * slope0[here, :]
        e = g_pre.astype(BF)
        gl[...] += mm(cb0_t[:, here], e)
        g_comb = (1.0 - MIX[0]) * g_pre + MIX[0] * mm(e, wl_t[0])
        ginit[here, :] += RESTART * g_comb
        gcb[1, here, :] = g_comb.astype(BF)

    scatter(1, MIX[0] * gl[...])
    gl[pl.ds(0, FIN), :] = jnp.zeros((FIN, WIDTH), F32)

    @pl.loop(0, ROWS // TILE)
    def _(t):
        here = pl.ds(pl.multiple_of(t * TILE, TILE), TILE)
        g_state = (1.0 - RESTART) * mm(adj_t[here, :], gcb[1])
        g_first = (ginit[here, :] + g_state) * slope_in[here, :]
        gl[pl.ds(0, FIN), :] += mm(feat_t[:, here], g_first.astype(BF))

    scatter(2, gl[pl.ds(0, FIN), :])
    exchange(0)
    exchange(1)
    exchange(2)
    gather(0)
    gather(1)
    gather(2)
    for part in range(3):
        for stage, buf in enumerate((plane_buf, crew_buf, plane_buf)):
            held = buf.at[part, pl.ds(0, buf.shape[1] - 1), :, lanes(part)]
            drain(held, sum_send.at[part, stage])
            if stage == 2:
                drain(held, sum_recv.at[part, stage])
    drain(idsend.at[pl.ds(0, DEVICES - 1)], id_send)
    drain(send.at[0, pl.ds(0, DEVICES - 1)], row_send.at[0])
    drain(send.at[1, pl.ds(0, DEVICES - 1)], row_send.at[1])
    fresh0.wait()
    fresh1.wait()
    final.wait()


def finish(
    fin, fresh, gsum, fin_out, fresh_out, grad_in, grad_layers,
    fin_held, fresh_held, gsum_held, first, layers, in_sem, out_sem,
):
    loads = [
        pltpu.make_async_copy(src, dst, in_sem.at[i])
        for i, (src, dst) in enumerate(
            [
                (gsum, gsum_held), (fin, fin_held), (fresh.at[0], fresh_held.at[0]),
                (fresh.at[1], fresh_held.at[1]),
            ]
        )
    ]
    stores = [
        pltpu.make_async_copy(src, dst, out_sem.at[i])
        for i, (src, dst) in enumerate(
            [
                (first, grad_in), (layers, grad_layers), (fin_held, fin_out),
                (fresh_held.at[0], fresh_out.at[0]), (fresh_held.at[1], fresh_out.at[1]),
            ]
        )
    ]
    for load in loads:
        load.start()
    factor = 1.0 / math.sqrt(ROWS * DEVICES)
    loads[0].wait()
    layers[0] = gsum_held[pl.ds(WIDTH, WIDTH), :].astype(F32) * factor
    layers[1] = gsum_held[pl.ds(0, WIDTH), :].astype(F32) * factor
    first[...] = gsum_held[pl.ds(2 * WIDTH, FIN), :].astype(F32) * factor
    stores[0].start()
    stores[1].start()
    for load, store in zip(loads[1:], stores[2:]):
        load.wait()
        store.start()
    for store in stores:
        store.wait()


def local(
    features, adjacency, halo_weights, history, pull_ids, pull_count, w_in, w_layers, cotangent
):
    anywhere = pl.BlockSpec(memory_space=pl.ANY)
    vmem = pltpu.VMEM
    dma = pltpu.SemaphoreType.DMA
    final_out, fresh, gsum = pl.pallas_call(
        kernel,
        out_shape=(
            jax.ShapeDtypeStruct((ROWS, WIDTH), BF),
            jax.ShapeDtypeStruct((2, ROWS, WIDTH), BF),
            jax.ShapeDtypeStruct((2 * WIDTH + FIN, WIDTH), BF),
        ),
        in_specs=[anywhere] * 9,
        out_specs=(anywhere, anywhere, pl.BlockSpec(memory_space=vmem)),
        scratch_shapes=[
            vmem((ROWS, FIN), BF),
            vmem((ROWS, ROWS), BF),
            vmem((ROWS, HALO), BF),
            vmem((2, ROWS, WIDTH), BF),
            vmem((SLOTS, DEVICES), jnp.int32),
            vmem((1, DEVICES), jnp.int32),
            vmem((FIN, WIDTH), BF),
            vmem((2, WIDTH, WIDTH), BF),
            vmem((ROWS, WIDTH), F32),
            vmem((DEVICES, 128), jnp.int32),
            vmem((DEVICES, 128), jnp.int32),
            vmem((DEVICES // GROUP, GROUP * SLOTS, ROWS), BF),
            vmem((2, DEVICES, 2 * SLOTS, 128), BF),
            vmem((2, DEVICES, 2 * SLOTS, 128), BF),
            vmem((HALO, WIDTH), BF),
            vmem((ROWS, WIDTH), BF),
            vmem((ROWS, WIDTH), BF),
            vmem((ROWS, WIDTH), BF),
            vmem((ROWS, ROWS), BF),
            vmem((FIN, ROWS), BF),
            vmem((2, WIDTH, WIDTH), BF),
            vmem((WIDTH, ROWS), BF),
            vmem((ROWS, WIDTH), F32),
            vmem((ROWS, WIDTH), F32),
            vmem((ROWS, WIDTH), F32),
            vmem((ROWS, WIDTH), F32),
            vmem((2, ROWS, WIDTH), BF),
            vmem((WIDTH, WIDTH), F32),
            vmem((2 * WIDTH + FIN, WIDTH), BF),
            vmem((3, 16, 16, WIDTH), BF),
            vmem((3, 8, 16, WIDTH), BF),
            dma((9,)),
            dma((3,)),
            dma(()),
            dma((8,)),
            dma((2,)),
            dma((5,)),
            dma((3, 3)),
            dma((3, 3)),
        ],
        compiler_params=pltpu.CompilerParams(
            collective_id=0, has_side_effects=True, vmem_limit_bytes=VMEM_LIMIT
        ),
    )(
        features, adjacency, halo_weights, history, pull_ids.T, pull_count, w_in, w_layers, cotangent
    )
    return pl.pallas_call(
        finish,
        out_shape=(
            jax.ShapeDtypeStruct((ROWS, WIDTH), BF),
            jax.ShapeDtypeStruct((2, ROWS, WIDTH), BF),
            jax.ShapeDtypeStruct((FIN, WIDTH), F32),
            jax.ShapeDtypeStruct((2, WIDTH, WIDTH), F32),
        ),
        in_specs=[anywhere] * 3,
        out_specs=(anywhere,) * 4,
        scratch_shapes=[
            vmem((ROWS, WIDTH), BF),
            vmem((2, ROWS, WIDTH), BF),
            vmem((2 * WIDTH + FIN, WIDTH), BF),
            vmem((FIN, WIDTH), F32),
            vmem((2, WIDTH, WIDTH), F32),
            dma((4,)),
            dma((5,)),
        ],
        compiler_params=pltpu.CompilerParams(vmem_limit_bytes=VMEM_LIMIT),
    )(final_out, fresh, gsum)


def solution(mesh):
    rows = P(("dom", "rep"), None)
    history = P(None, ("dom", "rep"), None)
    return jax.shard_map(
        local,
        mesh=mesh,
        in_specs=(rows, rows, rows, history, rows, rows, P(), P(), rows),
        out_specs=(rows, history, P(), P()),
        check_vma=False,
    )
```
